512 devices in a mesh: dp: 32 (over z, y_hi), tm: 4 (over y_lo, core), mp: 4 (over x).
Axes of the slice: x: 4, y: 4 (y_hi: 2, y_lo: 2; y = y_hi * 2 + y_lo), z: 16, core: 2. Of those that a mesh axis runs over, the one named last changes fastest.
Arguments:
- activations: bfloat16 [32, 8, 5, 40, 1280], P('dp', 'tm', None, None, 'mp'), may hold values from -1200 to 1200
- norm_gain: float32 [1280], P('mp'), may hold values from 0.25 to 1.75
- norm_bias: float32 [1280], P('mp'), may hold values from -3 to 3
- spatial_weight: bfloat16 [9, 1280, 1280], P(None, 'mp', 'tm'), may hold values from -0.0546875 to 0.0546875
- temporal_weight: bfloat16 [3, 1280, 1280], P(None, 'tm', 'mp'), may hold values from -0.09375 to 0.09375
- cotangent: bfloat16 [32, 8, 5, 40, 1280], P('dp', 'tm', None, None, 'mp'), may hold values from -6 to 6
Outputs:
- block_output: bfloat16 [32, 8, 5, 40, 1280], P('dp', 'tm', None, None, 'mp')
- temporal_grad: float32 [3, 1280, 1280], P(None, 'tm', 'mp')
The draws below stay inside these ranges and needn't reach their ends.
All inputs are finite; a program needn't handle non-finite values.
Results may differ from the reference program's by a relative error of at most 0.0058.
Values may be sent and summed in bfloat16 or wider, within the bound.
A program may use at most 64 MiB of HBM per device.

```python
import math
import jax
import jax.numpy as jnp
from jax import lax

CHANNELS = 1280
GROUPS = 32
ROWS_BAND = 5
COLUMNS = 40
FRAMES = 8
CLIPS = 32


def draw_activations(key, part):
    subkeys = jax.random.split(key, 3)
    shape = (CLIPS, FRAMES, ROWS_BAND, COLUMNS, CHANNELS)
    position_scale = jnp.exp(jax.random.uniform(subkeys[1], (CLIPS, FRAMES, ROWS_BAND, COLUMNS, 1), jnp.float32, 0.0, math.log(10.0)))
    channel_scale = jnp.exp(jax.random.uniform(subkeys[2], (CLIPS, 1, 1, 1, CHANNELS), jnp.float32, 0.0, math.log(10.0)))
    frame_index = jnp.arange(FRAMES, dtype=jnp.float32) / max(FRAMES - 1, 1)
    frame_scale = jnp.power(3.0, frame_index).reshape(1, FRAMES, 1, 1, 1)
    normal_part = jnp.clip(jax.random.normal(subkeys[0], shape, jnp.float32), -4.0, 4.0)
    values = normal_part * position_scale * channel_scale * frame_scale
    return values.astype(jnp.bfloat16)


def levels(own_key, shape, cuts, smallest, top_value):
    level = 1.0
    for axis_at, parts in cuts:
        draws = jax.random.uniform(jax.random.fold_in(jax.random.fold_in(own_key, 6), axis_at), (parts,), jnp.float32, smallest / len(cuts), top_value / len(cuts))
        level = level * jnp.repeat(jnp.exp(draws), shape[axis_at] // parts).reshape((-1,) + (1,) * (len(shape) - 1 - axis_at))
    return level


def scatter_about(rng, shape, scale, bound, cuts=(), held_as=jnp.bfloat16):
    drawn = scale * jax.random.normal(rng, shape, jnp.float32)
    if cuts:
        drawn = drawn * levels(rng, shape, cuts, -0.22, 0.18)
    return jnp.clip(drawn, -bound, bound).astype(held_as)


def setup_inputs(seed: int = 0) -> dict:
    key_of = jax.random.split(jax.random.key(seed), 7)
    return {
        "activations": draw_activations(jax.random.fold_in(key_of[6], 71), 0),
        "norm_gain": jnp.clip(1.0 + 0.15 * jax.random.normal(key_of[1], (CHANNELS,), jnp.float32), 0.25, 1.75),
        "norm_bias": scatter_about(key_of[2], (CHANNELS,), 0.5, 3.0, ((0, 4),), jnp.float32),
        "spatial_weight": scatter_about(key_of[3], (9, CHANNELS, CHANNELS), (9 * CHANNELS) ** -0.5, 0.0546875, ((1, 4), (2, 4))),
        "temporal_weight": scatter_about(key_of[4], (3, CHANNELS, CHANNELS), (3 * CHANNELS) ** -0.5, 0.09375, ((1, 4), (2, 4))),
        "cotangent": scatter_about(key_of[5], (CLIPS, FRAMES, ROWS_BAND, COLUMNS, CHANNELS), 1.0, 6.0, ((0, 32), (1, 4), (4, 4))),
    }


epsilon = 1e-05

def group_silu(clip_values, norm_gain, norm_bias):
    values = clip_values.astype(jnp.float32)
    shaped = values.reshape(values.shape[:3] + (GROUPS, CHANNELS // GROUPS))
    average = lax.optimization_barrier(jnp.mean(shaped, axis=(0, 1, 2, 4), keepdims=True))
    centered = shaped - average
    variance = lax.optimization_barrier(jnp.mean(centered * centered, axis=(0, 1, 2, 4), keepdims=True))
    normed = (centered * lax.rsqrt(variance + epsilon)).reshape(values.shape) * norm_gain + norm_bias
    return jax.nn.silu(normed).astype(jnp.bfloat16)

def spatial_conv(hidden, spatial_weight):
    padded = jnp.pad(hidden, ((0, 0), (1, 1), (1, 1), (0, 0)))
    summed = jnp.zeros((FRAMES * ROWS_BAND * COLUMNS, CHANNELS), jnp.float32)
    for tap_index in range(9):
        row_shift = tap_index // 3
        col_shift = tap_index % 3
        window = padded[:, row_shift:row_shift + ROWS_BAND, col_shift:col_shift + COLUMNS, :].reshape(-1, CHANNELS)
        summed = summed + jnp.dot(window, spatial_weight[tap_index], preferred_element_type=jnp.float32)
    return summed.reshape(FRAMES, ROWS_BAND, COLUMNS, CHANNELS).astype(jnp.bfloat16)

def reference(activations, norm_gain, norm_bias, spatial_weight, temporal_weight, cotangent):

    def per_clip(running, clip_pair):
        clip_values, clip_grad = clip_pair
        hidden = group_silu(clip_values, norm_gain, norm_bias)
        spatial = spatial_conv(hidden, spatial_weight)
        spatial_pad = jnp.pad(spatial, ((1, 1), (0, 0), (0, 0), (0, 0)))
        summed = jnp.zeros((FRAMES * ROWS_BAND * COLUMNS, CHANNELS), jnp.float32)
        flat_grad = clip_grad.reshape(-1, CHANNELS)
        tap_terms = []
        for tap_index in range(3):
            window = spatial_pad[tap_index:tap_index + FRAMES].reshape(-1, CHANNELS)
            summed = summed + jnp.dot(window, temporal_weight[tap_index], preferred_element_type=jnp.float32)
            tap_terms.append(lax.dot_general(window, flat_grad, (((0,), (0,)), ((), ())), preferred_element_type=jnp.float32))
        produced = summed.reshape(FRAMES, ROWS_BAND, COLUMNS, CHANNELS).astype(jnp.bfloat16)
        return (running + jnp.stack(tap_terms), produced)
    start_value = jnp.zeros((3, CHANNELS, CHANNELS), jnp.float32)
    grad_total, outputs = lax.scan(per_clip, start_value, (activations, cotangent))
    return (outputs, grad_total / CLIPS)
```

```python
import jax
import jax.numpy as jnp
from jax import lax
from jax.experimental import pallas as pl
from jax.experimental.pallas import tpu as pltpu
from jax.sharding import PartitionSpec as P

MESH = pl.DeviceIdType.MESH
F32, BF16 = jnp.float32, jnp.bfloat16

CH = 320
GROUP = 40
ROWS, COLS, PCOLS = 5, 40, 48
FR = ROWS * COLS
FP = 208
CUT = 112
HR = ROWS * PCOLS
CHUNK = 64
EPS = 1e-05


def dot(a, b, **kw):
    return jnp.dot(a, b, preferred_element_type=F32, **kw)


def kernel(
    act, gain, bias, ws, wt, cot, out, gout,
    actv, cotv, wsv, wtv, stats, hid, cotp, part, far_r, far_l, near, spat,
    grad, s1r, s2r, s1l, s2l, r1r, r2r, r1l, r2l, yhs, yhr, gath,
    tpre, tsame, tsend0, tsend1, ysend, yrecv, lsem, ssem, rsem,
):
    dp, tm, mp = lax.axis_index("dp"), lax.axis_index("tm"), lax.axis_index("mp")
    core, yl = lax.rem(tm, 2), lax.div(tm, 2)
    z, yh = lax.div(dp, 2), lax.rem(dp, 2)
    tc = tm + 1 - 2 * core
    ty = lax.rem(tm + 2, 4)
    tyc = lax.rem(tc + 2, 4)

    def zdev(s):
        return {"dp": lax.rem(dp + (2 * s + 32), 32)}

    def xdev(s):
        return {"mp": lax.rem(mp + (s + 4), 4)}

    names = {}

    def rc(name, src, dst, dev):
        i = names.setdefault(name, len(names))
        return pltpu.make_async_remote_copy(
            src_ref=src, dst_ref=dst, send_sem=ssem.at[i], recv_sem=rsem.at[i],
            device_id=dev, device_id_type=MESH,
        )

    started = []

    def send(name, src, dst, dev):
        c = rc(name, src, dst, dev)
        c.start()
        started.append(c)

    def arrived(name, dst, dev):
        rc(name, dst, dst, dev).wait_recv()

    c_act = pltpu.make_async_copy(act, actv, lsem.at[0])
    c_ws = pltpu.make_async_copy(ws, wsv, lsem.at[1])
    c_cot = pltpu.make_async_copy(cot, cotv, lsem.at[2])
    c_wt = pltpu.make_async_copy(wt, wtv, lsem.at[3])
    for c in (c_act, c_ws, c_cot, c_wt):
        c.start()
    yhd = {"dp": dp + 1 - 2 * yh}
    peers = [{"tm": tc}, {"tm": ty}, {"tm": tyc}, xdev(1), xdev(-1)]
    peers += [zdev(1), zdev(-1), zdev(2), zdev(-2), yhd]
    barrier = pltpu.get_barrier_semaphore()
    for p in peers:
        pl.semaphore_signal(barrier, inc=1, device_id=p, device_id_type=MESH)

    zrows = jnp.zeros((8, PCOLS, CH), BF16)
    hid[:, pl.ds(0, PCOLS), :] = zrows
    hid[:, pl.ds(PCOLS + HR, PCOLS), :] = zrows
    spat[pl.ds(0, FP), :] = jnp.zeros((FP, CH), BF16)
    spat[pl.ds(9 * FP, FP), :] = jnp.zeros((FP, CH), BF16)
    grad[15] = jnp.zeros((CHUNK, CH), F32)

    c_act.wait()
    x = actv[...].astype(F32).reshape(2 * FR, CH)
    ssum = jnp.sum(x, axis=0, keepdims=True)
    cen = x - ssum * (1.0 / (2 * FR))
    m2 = jnp.sum(cen * cen, axis=0, keepdims=True)
    r8 = lax.broadcasted_iota(jnp.int32, (8, CH), 0)
    stats[tm] = jnp.where(r8 == 0, ssum, jnp.where(r8 == 1, m2, 0.0))

    pl.semaphore_wait(barrier, len(peers))
    send("st_c", stats.at[tm], stats.at[tm], {"tm": tc})
    send("st_y", stats.at[tm], stats.at[tm], {"tm": ty})
    send("st_yc", stats.at[tm], stats.at[tm], {"tm": tyc})

    gi = lax.broadcasted_iota(jnp.int32, (CH, CH), 0)
    gj = lax.broadcasted_iota(jnp.int32, (CH, CH), 1)
    same = (((gi * 1639) >> 16) == ((gj * 1639) >> 16)).astype(F32)

    c_cot.wait()
    zpad = jnp.zeros((FP - FR, CH), F32)
    for i in range(2):
        cf = cotv[0, i].astype(F32).reshape(FR, CH)
        cotp[pl.ds(pl.multiple_of((2 * tm + i) * FP, FP), FP), :] = jnp.concatenate(
            [cf, zpad], axis=0
        ).astype(BF16)

    arrived("st_c", stats.at[tc], {"tm": tc})
    arrived("st_y", stats.at[ty], {"tm": ty})
    arrived("st_yc", stats.at[tyc], {"tm": tyc})
    st = [stats[i] for i in range(4)]
    total = st[0] + st[1] + st[2] + st[3]
    hi = lax.Precision.HIGHEST
    avg = dot(total, same, precision=hi)[0:1] * (1.0 / (8 * FR * GROUP))
    m2all = total[1:2]
    for i in range(4):
        dm = st[i][0:1] * (1.0 / (2 * FR)) - avg
        m2all = m2all + (2.0 * FR) * dm * dm
    m2all = jnp.broadcast_to(m2all, (8, CH))
    var = dot(m2all, same, precision=hi)[0:1] * (1.0 / (8 * FR * GROUP))
    inv = lax.rsqrt(var + EPS) * gain[...]
    bia = bias[...]

    for i in range(2):
        xf = actv[0, i].astype(F32).reshape(FR, CH)
        nf = (xf - avg) * inv + bia
        hf = nf * (1.0 / (1.0 + jnp.exp(-nf)))
        hf = jnp.concatenate(
            [hf.reshape(ROWS, COLS, CH), jnp.zeros((ROWS, PCOLS - COLS, CH), F32)], axis=1
        )
        hid[2 * tm + i, pl.ds(PCOLS, HR), :] = hf.reshape(HR, CH).astype(BF16)
        own = hid.at[2 * tm + i, pl.ds(PCOLS, HR), :]
        send(f"hy{i}", own, own, {"tm": ty})
        send(f"hc{i}", own, own, {"tm": tc})

    def cframes(t):
        return cotp.at[pl.ds(pl.multiple_of(2 * t * FP, FP), 2 * FP), :]

    send("cy", cframes(tm), cframes(tm), {"tm": ty})
    send("cc", cframes(tm), cframes(tm), {"tm": tc})

    def hframe(f):
        return hid.at[f, pl.ds(PCOLS, HR), :]

    def relay_hidden(i):
        return rc(f"hr{i}", hframe(2 * ty + i), hframe(2 * ty + i), {"tm": tc})

    def conv(f):
        acc = []
        for b in range(3):
            v = dot(hid[f, pl.ds(0, HR), :], wsv[b])
            for a in (1, 2):
                v = v + dot(hid[f, pl.ds(PCOLS * a, HR), :], wsv[3 * a + b])
            acc.append(v)
        o = acc[1] + pltpu.roll(acc[0], 1, 0) + pltpu.roll(acc[2], HR - 1, 0)
        o = o.reshape(ROWS, PCOLS, CH)[:, :COLS, :].reshape(FR, CH)
        return jnp.concatenate([o, zpad], axis=0)

    def sframe(f):
        return pl.ds(pl.multiple_of((f + 1) * FP, FP), FP)

    top, low = pl.ds(0, CUT), pl.ds(CUT, FP - CUT)

    def half_sums(h, base, extra):
        def step(j, _):
            q, r = lax.div(j, 2), lax.rem(j, 2)
            off = 2 + q - r - 2 * q * r
            val = conv(base + lax.rem(mp + off, 4))

            @pl.when(j == 0)
            def _():
                part[h, 0] = val.astype(BF16)
                rc(f"fr{h}", part.at[h, 0, top], far_r.at[h], xdev(1)).start()
                rc(f"fl{h}", part.at[h, 0, low], far_l.at[h], xdev(-1)).start()

            @pl.when(j == 1)
            def _():
                arrived(f"fr{h}", far_r.at[h], xdev(-1))
                up = val[:CUT] + far_r[h].astype(F32)
                part[h, 1, top] = up.astype(BF16)
                part[h, 1, low] = val[CUT:].astype(BF16)
                rc(f"nr{h}", part.at[h, 1], near.at[h, 0], xdev(1)).start()

            @pl.when(j == 2)
            def _():
                arrived(f"fl{h}", far_l.at[h], xdev(1))
                dn = val[CUT:] + far_l[h].astype(F32)
                part[h, 2, top] = val[:CUT].astype(BF16)
                part[h, 2, low] = dn.astype(BF16)
                rc(f"nl{h}", part.at[h, 2], near.at[h, 1], xdev(-1)).start()

            @pl.when(j == 3)
            def _():
                extra()
                arrived(f"nr{h}", near.at[h, 0], xdev(-1))
                arrived(f"nl{h}", near.at[h, 1], xdev(1))
                whole = val + near[h, 0].astype(F32) + near[h, 1].astype(F32)
                spat[sframe(base + mp), :] = whole.astype(BF16)

            return 0

        lax.fori_loop(0, 4, step, 0)
        started.append(rc(f"fr{h}", part.at[h, 0, top], far_r.at[h], xdev(1)))
        started.append(rc(f"fl{h}", part.at[h, 0, low], far_l.at[h], xdev(-1)))
        started.append(rc(f"nr{h}", part.at[h, 1], near.at[h, 0], xdev(1)))
        started.append(rc(f"nl{h}", part.at[h, 2], near.at[h, 1], xdev(-1)))
        mine = spat.at[sframe(base + mp), :]
        send(f"gr{h}", mine, mine, xdev(1))
        send(f"gl{h}", mine, mine, xdev(-1))

    def spart(f, lo, n):
        return spat.at[pl.ds(pl.multiple_of((f + 1) * FP + lo, 16), n), :]

    def forwards(h, base):
        lf, rf = base + lax.rem(mp + 3, 4), base + lax.rem(mp + 1, 4)
        return (
            rc(f"wr{h}", spart(lf, 0, CUT), spart(lf, 0, CUT), xdev(1)),
            rc(f"wl{h}", spart(rf, CUT, FP - CUT), spart(rf, CUT, FP - CUT), xdev(-1)),
        )

    def half_forward(h, base):
        lf, rf = base + lax.rem(mp + 3, 4), base + lax.rem(mp + 1, 4)
        to_r, to_l = forwards(h, base)
        arrived(f"gr{h}", spat.at[sframe(lf), :], xdev(-1))
        to_r.start()
        arrived(f"gl{h}", spat.at[sframe(rf), :], xdev(1))
        to_l.start()

    def half_done(h, base):
        ff = base + lax.rem(mp + 2, 4)
        arrived(f"wr{h}", spart(ff, 0, CUT), xdev(-1))
        arrived(f"wl{h}", spart(ff, CUT, FP - CUT), xdev(1))

    base0, base1 = 4 * yl, 4 * (1 - yl)
    c_ws.wait()
    for i in range(2):
        arrived(f"hc{i}", hframe(2 * tc + i), {"tm": tc})

    def relay_both():
        for i in range(2):
            arrived(f"hy{i}", hframe(2 * ty + i), {"tm": ty})
            relay_hidden(i).start()

    half_sums(0, base0, relay_both)
    for i in range(2):
        started.append(relay_hidden(i))
        arrived(f"hr{i}", hframe(2 * tyc + i), {"tm": tc})

    def between():
        half_forward(0, base0)

    half_sums(1, base1, between)
    arrived("cc", cframes(tc), {"tm": tc})
    arrived("cy", cframes(ty), {"tm": ty})
    send("cr", cframes(ty), cframes(ty), {"tm": tc})
    half_forward(1, base1)
    started.extend(forwards(0, base0))
    started.extend(forwards(1, base1))
    arrived("cr", cframes(tyc), {"tm": tc})
    half_done(0, base0)
    half_done(1, base1)
    c_wt.wait()

    for k in range(3):
        g = lax.dot_general(
            spat[pl.ds(k * FP, 8 * FP), :], cotp[...], (((0,), (0,)), ((), ())),
            preferred_element_type=F32,
        )
        grad[pl.ds(5 * k, 5)] = g.reshape(5, CHUNK, CH)

    def own(s):
        return grad[lax.rem(z + (s + 16), 16)]

    s2r[0] = own(8).astype(BF16)
    send("zr0", s2r.at[0], r2r.at[0], zdev(2))
    for i in (3, 2, 1, 0):
        s1r[i] = own(2 * i + 1).astype(BF16)
        send(f"or{i}", s1r.at[i], r1r.at[i], zdev(1))
        s1l[i] = own(-2 * i - 1).astype(BF16)
        send(f"ol{i}", s1l.at[i], r1l.at[i], zdev(-1))

    def temporal(t):
        r0 = pl.multiple_of(2 * t * FP, FP)
        v = dot(spat[pl.ds(r0, 2 * FP), :], wtv[0])
        for k in (1, 2):
            v = v + dot(spat[pl.ds(pl.multiple_of(r0 + k * FP, FP), 2 * FP), :], wtv[k])
        return v

    tsend0[...] = temporal(tyc)
    send("tp", tsend0, tpre, {"tm": tc})

    def chain_r(i):
        arrived(f"or{4 - i}", r1r.at[4 - i], zdev(-1))
        arrived(f"zr{i - 1}", r2r.at[i - 1], zdev(-2))
        v = own(8 - 2 * i) + r1r[4 - i].astype(F32) + r2r[i - 1].astype(F32)
        if i < 4:
            s2r[i] = v.astype(BF16)
            send(f"zr{i}", s2r.at[i], r2r.at[i], zdev(2))
        return v

    def chain_l(i):
        arrived(f"ol{3 - i}", r1l.at[3 - i], zdev(1))
        v = r1l[3 - i].astype(F32)
        if i > 0:
            arrived(f"zl{i - 1}", r2l.at[i - 1], zdev(2))
            v = v + r2l[i - 1].astype(F32)
        if i < 3:
            s2l[i] = (own(-6 + 2 * i) + v).astype(BF16)
            send(f"zl{i}", s2l.at[i], r2l.at[i], zdev(-2))
        return v

    chain_l(0)
    chain_r(1)
    tsend1[...] = temporal(tc)
    send("ts", tsend1, tsame, {"tm": tc})
    chain_l(1)
    chain_r(2)
    tacc = temporal(ty)
    arrived("tp", tpre, {"tm": tc})
    ysend[...] = (tacc + tpre[...]).astype(BF16)
    send("ty", ysend, yrecv, {"tm": ty})
    chain_l(2)
    chain_r(3)
    tsend_own = temporal(tm)
    arrived("ts", tsame, {"tm": tc})
    tsame[...] = tsame[...] + tsend_own
    yhs[...] = chain_l(3) + chain_r(4)
    send("yh", yhs, yhr, yhd)
    arrived("yh", yhr, yhd)
    gath[z] = ((yhs[...] + yhr[...]) * (1.0 / 32.0)).astype(BF16)

    def slot(s):
        return gath.at[lax.rem(z + (s + 32), 16)]

    send("ar0", slot(0), slot(0), zdev(2))
    send("al0", slot(0), slot(0), zdev(-2))
    send("br0", slot(0), slot(0), zdev(1))
    send("bl0", slot(0), slot(0), zdev(-1))
    arrived("ty", yrecv, {"tm": ty})
    res = tsame[...] + yrecv[...].astype(F32)
    for i in range(2):
        out[0, i] = res[i * FP : i * FP + FR].reshape(ROWS, COLS, CH).astype(BF16)
    for i in (1, 2, 3):
        arrived(f"ar{i - 1}", slot(-2 * i), zdev(-2))
        send(f"ar{i}", slot(-2 * i), slot(-2 * i), zdev(2))
        arrived(f"al{i - 1}", slot(2 * i), zdev(2))
        if i < 3:
            send(f"al{i}", slot(2 * i), slot(2 * i), zdev(-2))
        send(f"br{i}", slot(-2 * i), slot(-2 * i), zdev(1))
        send(f"bl{i}", slot(2 * i), slot(2 * i), zdev(-1))
    arrived("ar3", slot(-8), zdev(-2))
    for i in range(4):
        arrived(f"br{i}", slot(-2 * i - 1), zdev(-1))
        arrived(f"bl{i}", slot(2 * i + 1), zdev(1))
    for i in range(15):
        gout[pl.ds(i * CHUNK, CHUNK), :] = gath[i].astype(F32)
    for c in started:
        c.wait_send()


def body(activations, norm_gain, norm_bias, spatial_weight, temporal_weight, cotangent):
    anyspec = pl.BlockSpec(memory_space=pl.ANY)
    vm = pl.BlockSpec(memory_space=pltpu.VMEM)
    V = pltpu.VMEM
    zc = (CHUNK, CH)
    scratch = [
        V((1, 2, ROWS, COLS, CH), BF16),
        V((1, 2, ROWS, COLS, CH), BF16),
        V((9, CH, CH), BF16),
        V((3, CH, CH), BF16),
        V((4, 8, CH), F32),
        V((8, HR + 2 * PCOLS, CH), BF16),
        V((8 * FP, CH), BF16),
        V((2, 3, FP, CH), BF16),
        V((2, CUT, CH), BF16),
        V((2, FP - CUT, CH), BF16),
        V((2, 2, FP, CH), BF16),
        V((10 * FP, CH), BF16),
        V((16,) + zc, F32),
        V((4,) + zc, BF16),
        V((4,) + zc, BF16),
        V((4,) + zc, BF16),
        V((3,) + zc, BF16),
        V((4,) + zc, BF16),
        V((4,) + zc, BF16),
        V((4,) + zc, BF16),
        V((3,) + zc, BF16),
        V(zc, F32),
        V(zc, F32),
        V((16,) + zc, BF16),
        V((2 * FP, CH), F32),
        V((2 * FP, CH), F32),
        V((2 * FP, CH), F32),
        V((2 * FP, CH), F32),
        V((2 * FP, CH), BF16),
        V((2 * FP, CH), BF16),
        pltpu.SemaphoreType.DMA((4,)),
        pltpu.SemaphoreType.DMA((80,)),
        pltpu.SemaphoreType.DMA((80,)),
    ]
    out, gout = pl.pallas_call(
        kernel,
        out_shape=(
            jax.ShapeDtypeStruct((1, 2, ROWS, COLS, CH), BF16),
            jax.ShapeDtypeStruct((3 * CH, CH), F32),
        ),
        in_specs=[anyspec, vm, vm, anyspec, anyspec, anyspec],
        out_specs=(vm, vm),
        scratch_shapes=scratch,
        compiler_params=pltpu.CompilerParams(
            collective_id=0, has_side_effects=True, vmem_limit_bytes=48 * 2**20
        ),
        name="block",
    )(
        activations,
        norm_gain.reshape(1, CH),
        norm_bias.reshape(1, CH),
        spatial_weight,
        temporal_weight,
        cotangent,
    )
    return out, gout.reshape(3, CH, CH)


def solution(mesh):
    in_specs = (
        P("dp", "tm", None, None, "mp"),
        P("mp"),
        P("mp"),
        P(None, "mp", "tm"),
        P(None, "tm", "mp"),
        P("dp", "tm", None, None, "mp"),
    )
    out_specs = (P("dp", "tm", None, None, "mp"), P(None, "tm", "mp"))
    return jax.shard_map(body, mesh=mesh, in_specs=in_specs, out_specs=out_specs, check_vma=False)
```

```python
import jax
import jax.numpy as jnp
from jax import lax
from jax.experimental import pallas as pl
from jax.experimental.pallas import tpu as pltpu
from jax.sharding import PartitionSpec as P

MESH = pl.DeviceIdType.MESH
F32, BF16 = jnp.float32, jnp.bfloat16

CH = 320
GROUP = 40
ROWS, COLS, PCOLS = 5, 40, 48
FR = ROWS * COLS
FP = 208
CUT = 112
HR = ROWS * PCOLS
ZR = 160
EPS = 1e-05


def dot(a, b, **kw):
    return jnp.dot(a, b, preferred_element_type=F32, **kw)


def kernel(
    act, gain, bias, ws, wt, cot, out, gout,
    actv, cotv, wsv, wtv, gainv, biasv, stats, hid, cotp, part, far_r, far_l, near, spat,
    grad, s1r, s2r, s1l, s2l, r1r, r2r, r1l, r2l, yhs, yhr, gath, hold, mine,
    tpre, tsame, tsend0, tsend1, ysend, yrecv, lsem, ssem, rsem,
):
    dp, tm, mp = lax.axis_index("dp"), lax.axis_index("tm"), lax.axis_index("mp")
    core, yl = lax.rem(tm, 2), lax.div(tm, 2)
    z, yh = lax.div(dp, 2), lax.rem(dp, 2)
    tc = tm + 1 - 2 * core
    ty = lax.rem(tm + 2, 4)
    tyc = lax.rem(tc + 2, 4)

    def zdev(s):
        return {"dp": lax.rem(dp + (2 * s + 32), 32)}

    def xdev(s):
        return {"mp": lax.rem(mp + (s + 4), 4)}

    names = {}

    def rc(name, src, dst, dev):
        i = names.setdefault(name, len(names))
        return pltpu.make_async_remote_copy(
            src_ref=src, dst_ref=dst, send_sem=ssem.at[i], recv_sem=rsem.at[i],
            device_id=dev, device_id_type=MESH,
        )

    started = []

    def send(name, src, dst, dev):
        c = rc(name, src, dst, dev)
        c.start()
        started.append(c)

    def arrived(name, dst, dev):
        rc(name, dst, dst, dev).wait_recv()

    c_act = pltpu.make_async_copy(act, actv, lsem.at[0])
    c_ws = pltpu.make_async_copy(ws, wsv, lsem.at[1])
    c_cot = pltpu.make_async_copy(cot, cotv, lsem.at[2])
    c_wt = pltpu.make_async_copy(wt, wtv, lsem.at[3])
    c_gain = pltpu.make_async_copy(gain, gainv, lsem.at[4])
    c_bias = pltpu.make_async_copy(bias, biasv, lsem.at[5])
    for c in (c_act, c_gain, c_bias, c_cot, c_ws, c_wt):
        c.start()
    yhd = {"dp": dp + 1 - 2 * yh}
    peers = [{"tm": tc}, {"tm": ty}, {"tm": tyc}, xdev(1), xdev(-1)]
    peers += [zdev(1), zdev(-1), zdev(2), zdev(-2), yhd]
    barrier = pltpu.get_barrier_semaphore()
    for p in peers:
        pl.semaphore_signal(barrier, inc=1, device_id=p, device_id_type=MESH)

    zrows = jnp.zeros((8, PCOLS, CH), BF16)
    hid[:, pl.ds(0, PCOLS), :] = zrows
    hid[:, pl.ds(PCOLS + HR, PCOLS), :] = zrows
    spat[pl.ds(0, FP), :] = jnp.zeros((FP, CH), BF16)
    spat[pl.ds(9 * FP, FP), :] = jnp.zeros((FP, CH), BF16)
    grad[15] = jnp.zeros((ZR, 128), F32)

    c_act.wait()
    x = actv[...].astype(F32).reshape(2 * FR, CH)
    ssum = jnp.sum(x, axis=0, keepdims=True)
    cen = x - ssum * (1.0 / (2 * FR))
    m2 = jnp.sum(cen * cen, axis=0, keepdims=True)
    r8 = lax.broadcasted_iota(jnp.int32, (8, CH), 0)
    stats[tm] = jnp.where(r8 == 0, ssum, jnp.where(r8 == 1, m2, 0.0))

    pl.semaphore_wait(barrier, len(peers))
    send("st_c", stats.at[tm], stats.at[tm], {"tm": tc})
    send("st_y", stats.at[tm], stats.at[tm], {"tm": ty})
    send("st_yc", stats.at[tm], stats.at[tm], {"tm": tyc})

    gi = lax.broadcasted_iota(jnp.int32, (CH, CH), 0)
    gj = lax.broadcasted_iota(jnp.int32, (CH, CH), 1)
    same = (((gi * 1639) >> 16) == ((gj * 1639) >> 16)).astype(F32)

    c_cot.wait()
    zpad = jnp.zeros((FP - FR, CH), F32)
    for i in range(2):
        cf = cotv[0, i].astype(F32).reshape(FR, CH)
        cotp[pl.ds(pl.multiple_of((2 * tm + i) * FP, FP), FP), :] = jnp.concatenate(
            [cf, zpad], axis=0
        ).astype(BF16)

    arrived("st_c", stats.at[tc], {"tm": tc})
    arrived("st_y", stats.at[ty], {"tm": ty})
    arrived("st_yc", stats.at[tyc], {"tm": tyc})
    st = [stats[i] for i in range(4)]
    total = st[0] + st[1] + st[2] + st[3]
    hi = lax.Precision.HIGHEST
    avg = dot(total, same, precision=hi)[0:1] * (1.0 / (8 * FR * GROUP))
    m2all = total[1:2]
    for i in range(4):
        dm = st[i][0:1] * (1.0 / (2 * FR)) - avg
        m2all = m2all + (2.0 * FR) * dm * dm
    m2all = jnp.broadcast_to(m2all, (8, CH))
    var = dot(m2all, same, precision=hi)[0:1] * (1.0 / (8 * FR * GROUP))
    c_gain.wait()
    c_bias.wait()
    inv = lax.rsqrt(var + EPS) * gainv[...].reshape(1, CH)
    bia = biasv[...].reshape(1, CH)

    for i in range(2):
        xf = actv[0, i].astype(F32).reshape(FR, CH)
        nf = (xf - avg) * inv + bia
        hf = nf * (1.0 / (1.0 + jnp.exp(-nf)))
        hf = jnp.concatenate(
            [hf.reshape(ROWS, COLS, CH), jnp.zeros((ROWS, PCOLS - COLS, CH), F32)], axis=1
        )
        hid[2 * tm + i, pl.ds(PCOLS, HR), :] = hf.reshape(HR, CH).astype(BF16)
        own = hid.at[2 * tm + i, pl.ds(PCOLS, HR), :]
        send(f"hy{i}", own, own, {"tm": ty})
        send(f"hc{i}", own, own, {"tm": tc})

    def cframes(t):
        return cotp.at[pl.ds(pl.multiple_of(2 * t * FP, FP), 2 * FP), :]

    def hframe(f):
        return hid.at[f, pl.ds(PCOLS, HR), :]

    def relay_hidden(i):
        return rc(f"hr{i}", hframe(2 * ty + i), hframe(2 * ty + i), {"tm": tc})

    def conv(f):
        acc = []
        for b in range(3):
            v = dot(hid[f, pl.ds(0, HR), :], wsv[b])
            for a in (1, 2):
                v = v + dot(hid[f, pl.ds(PCOLS * a, HR), :], wsv[3 * a + b])
            acc.append(v)
        o = acc[1] + pltpu.roll(acc[0], 1, 0) + pltpu.roll(acc[2], HR - 1, 0)
        o = o.reshape(ROWS, PCOLS, CH)[:, :COLS, :].reshape(FR, CH)
        return jnp.concatenate([o, zpad], axis=0)

    def sframe(f):
        return pl.ds(pl.multiple_of((f + 1) * FP, FP), FP)

    top, low = pl.ds(0, CUT), pl.ds(CUT, FP - CUT)

    def far(h):
        return (
            rc(f"fr{h}", part.at[h, 0, top], far_r.at[h], xdev(1)),
            rc(f"fl{h}", part.at[h, 0, low], far_l.at[h], xdev(-1)),
        )

    def near_early(h):
        return (
            rc(f"nrl{h}", part.at[h, 1, low], near.at[h, 0, low], xdev(1)),
            rc(f"nlt{h}", part.at[h, 2, top], near.at[h, 1, top], xdev(-1)),
        )

    def gathers(h, base):
        f = base + mp
        t, b = spart(f, 0, CUT), spart(f, CUT, FP - CUT)
        return (
            rc(f"grt{h}", t, t, xdev(1)),
            rc(f"glb{h}", b, b, xdev(-1)),
            rc(f"grb{h}", b, b, xdev(1)),
            rc(f"glt{h}", t, t, xdev(-1)),
        )

    def half_convs(h, base, hook):
        def step(j, _):
            q, r = lax.div(j, 2), lax.rem(j, 2)
            off = 2 + q - r - 2 * q * r
            hold[j] = conv(base + lax.rem(mp + off, 4))

            @pl.when(j == 0)
            def _():
                part[h, 0] = hold[0].astype(BF16)
                for c in far(h):
                    c.start()

            @pl.when(j == 1)
            def _():
                part[h, 1, low] = hold[1, low].astype(BF16)
                near_early(h)[0].start()

            @pl.when(j == 2)
            def _():
                part[h, 2, top] = hold[2, top].astype(BF16)
                near_early(h)[1].start()

            hook(j)
            return 0

        lax.fori_loop(0, 4, step, 0)
        started.extend(far(h))
        started.extend(near_early(h))

    def half_near(h):
        arrived(f"fr{h}", far_r.at[h], xdev(-1))
        part[h, 1, top] = (hold[1, top] + far_r[h].astype(F32)).astype(BF16)
        send(f"nrt{h}", part.at[h, 1, top], near.at[h, 0, top], xdev(1))
        arrived(f"fl{h}", far_l.at[h], xdev(1))
        part[h, 2, low] = (hold[2, low] + far_l[h].astype(F32)).astype(BF16)
        send(f"nll{h}", part.at[h, 2, low], near.at[h, 1, low], xdev(-1))
        mine[...] = hold[3]

    def half_sum(h, base):
        arrived(f"nrl{h}", near.at[h, 0, low], xdev(-1))
        arrived(f"nlt{h}", near.at[h, 1, top], xdev(1))
        arrived(f"nrt{h}", near.at[h, 0, top], xdev(-1))
        arrived(f"nll{h}", near.at[h, 1, low], xdev(1))
        whole = mine[...] + near[h, 0].astype(F32) + near[h, 1].astype(F32)
        spat[sframe(base + mp), :] = whole.astype(BF16)
        for c in gathers(h, base):
            c.start()

    def spart(f, lo, n):
        return spat.at[pl.ds(pl.multiple_of((f + 1) * FP + lo, 16), n), :]

    def forwards(h, base):
        lf, rf = base + lax.rem(mp + 3, 4), base + lax.rem(mp + 1, 4)
        return (
            rc(f"wr{h}", spart(lf, 0, CUT), spart(lf, 0, CUT), xdev(1)),
            rc(f"wl{h}", spart(rf, CUT, FP - CUT), spart(rf, CUT, FP - CUT), xdev(-1)),
        )

    def half_forward(h, base):
        lf, rf = base + lax.rem(mp + 3, 4), base + lax.rem(mp + 1, 4)
        to_r, to_l = forwards(h, base)
        arrived(f"grt{h}", spart(lf, 0, CUT), xdev(-1))
        to_r.start()
        arrived(f"glb{h}", spart(rf, CUT, FP - CUT), xdev(1))
        to_l.start()

    def half_done(h, base):
        lf, rf = base + lax.rem(mp + 3, 4), base + lax.rem(mp + 1, 4)
        ff = base + lax.rem(mp + 2, 4)
        arrived(f"grb{h}", spart(lf, CUT, FP - CUT), xdev(-1))
        arrived(f"glt{h}", spart(rf, 0, CUT), xdev(1))
        arrived(f"wr{h}", spart(ff, 0, CUT), xdev(-1))
        arrived(f"wl{h}", spart(ff, CUT, FP - CUT), xdev(1))

    base0, base1 = 4 * yl, 4 * (1 - yl)
    c_ws.wait()
    for i in range(2):
        arrived(f"hc{i}", hframe(2 * tc + i), {"tm": tc})

    half_convs(0, base0, lambda j: None)
    half_near(0)
    for i in range(2):
        arrived(f"hy{i}", hframe(2 * ty + i), {"tm": ty})
        c = relay_hidden(i)
        c.start()
        started.append(c)
    send("cy", cframes(tm), cframes(tm), {"tm": ty})
    for i in range(2):
        arrived(f"hr{i}", hframe(2 * tyc + i), {"tm": tc})

    def between(j):
        @pl.when(j == 1)
        def _():
            half_sum(0, base0)

    half_convs(1, base1, between)
    started.extend(gathers(0, base0))
    half_near(1)
    send("cc", cframes(tm), cframes(tm), {"tm": tc})
    half_forward(0, base0)
    started.extend(forwards(0, base0))
    half_sum(1, base1)
    started.extend(gathers(1, base1))
    arrived("cc", cframes(tc), {"tm": tc})
    arrived("cy", cframes(ty), {"tm": ty})
    send("cr", cframes(ty), cframes(ty), {"tm": tc})
    half_forward(1, base1)
    started.extend(forwards(1, base1))
    arrived("cr", cframes(tyc), {"tm": tc})
    half_done(0, base0)
    half_done(1, base1)
    c_wt.wait()

    tails = []
    for k in range(3):
        g = lax.dot_general(
            spat[pl.ds(k * FP, 8 * FP), :], cotp[...], (((0,), (0,)), ((), ())),
            preferred_element_type=F32,
        )
        for a in range(2):
            grad[pl.ds(4 * k + 2 * a, 2)] = g[:, 128 * a : 128 * a + 128].reshape(2, ZR, 128)
        tails.append(g[:, 256:])
    grad[pl.ds(12, 2)] = jnp.concatenate(tails[:2], axis=1).reshape(2, ZR, 128)
    grad[14] = jnp.concatenate([tails[2][:ZR], tails[2][ZR:]], axis=1)

    def own(s):
        return grad[lax.rem(z + (s + 16), 16)]

    def one_hop(i):
        s1r[i] = own(2 * i + 1).astype(BF16)
        s1l[i] = own(-2 * i - 1).astype(BF16)
        send(f"or{i}", s1r.at[i], r1r.at[i], zdev(1))
        send(f"ol{i}", s1l.at[i], r1l.at[i], zdev(-1))

    s2r[0] = own(8).astype(BF16)
    send("zr0", s2r.at[0], r2r.at[0], zdev(2))
    one_hop(3)

    def temporal(t):
        r0 = pl.multiple_of(2 * t * FP, FP)
        v = dot(spat[pl.ds(r0, 2 * FP), :], wtv[0])
        for k in (1, 2):
            v = v + dot(spat[pl.ds(pl.multiple_of(r0 + k * FP, FP), 2 * FP), :], wtv[k])
        return v

    tsend0[...] = temporal(tyc)
    send("tp", tsend0, tpre, {"tm": tc})

    def chain_r(i):
        arrived(f"or{4 - i}", r1r.at[4 - i], zdev(-1))
        arrived(f"zr{i - 1}", r2r.at[i - 1], zdev(-2))
        v = own(8 - 2 * i) + r1r[4 - i].astype(F32) + r2r[i - 1].astype(F32)
        if i < 4:
            s2r[i] = v.astype(BF16)
            send(f"zr{i}", s2r.at[i], r2r.at[i], zdev(2))
        return v

    def chain_l(i):
        arrived(f"ol{3 - i}", r1l.at[3 - i], zdev(1))
        v = r1l[3 - i].astype(F32)
        if i > 0:
            arrived(f"zl{i - 1}", r2l.at[i - 1], zdev(2))
            v = v + r2l[i - 1].astype(F32)
        if i < 3:
            s2l[i] = (own(-6 + 2 * i) + v).astype(BF16)
            send(f"zl{i}", s2l.at[i], r2l.at[i], zdev(-2))
        return v

    chain_l(0)
    chain_r(1)
    one_hop(2)
    tsend1[...] = temporal(tc)
    send("ts", tsend1, tsame, {"tm": tc})
    chain_l(1)
    chain_r(2)
    one_hop(1)
    tacc = temporal(ty)
    arrived("tp", tpre, {"tm": tc})
    ysend[...] = (tacc + tpre[...]).astype(BF16)
    send("ty", ysend, yrecv, {"tm": ty})
    chain_l(2)
    chain_r(3)
    one_hop(0)
    tsend_own = temporal(tm)
    arrived("ts", tsame, {"tm": tc})
    tsame[...] = tsame[...] + tsend_own
    yhs[...] = chain_l(3) + chain_r(4)
    send("yh", yhs, yhr, yhd)
    arrived("yh", yhr, yhd)
    gath[z] = ((yhs[...] + yhr[...]) * (1.0 / 32.0)).astype(BF16)

    def slot(s):
        return gath.at[lax.rem(z + (s + 32), 16)]

    send("ar0", slot(0), slot(0), zdev(2))
    send("al0", slot(0), slot(0), zdev(-2))
    send("br0", slot(0), slot(0), zdev(1))
    send("bl0", slot(0), slot(0), zdev(-1))
    arrived("ty", yrecv, {"tm": ty})
    res = tsame[...] + yrecv[...].astype(F32)
    for i in range(2):
        out[0, i] = res[i * FP : i * FP + FR].reshape(ROWS, COLS, CH).astype(BF16)
    for i in (1, 2, 3):
        arrived(f"ar{i - 1}", slot(-2 * i), zdev(-2))
        send(f"ar{i}", slot(-2 * i), slot(-2 * i), zdev(2))
        arrived(f"al{i - 1}", slot(2 * i), zdev(2))
        if i < 3:
            send(f"al{i}", slot(2 * i), slot(2 * i), zdev(-2))
        send(f"br{i}", slot(-2 * i), slot(-2 * i), zdev(1))
        send(f"bl{i}", slot(2 * i), slot(2 * i), zdev(-1))
    for i in range(4):
        arrived(f"br{i}", slot(-2 * i - 1), zdev(-1))
        arrived(f"bl{i}", slot(2 * i + 1), zdev(1))
    arrived("ar3", slot(-8), zdev(-2))
    for j in range(12):
        k, a, b = j // 4, j // 2 % 2, j % 2
        gout[k, pl.ds(b * ZR, ZR), pl.ds(128 * a, 128)] = gath[j].astype(F32)
    for b in range(2):
        v = gath[12 + b].astype(F32)
        gout[0, pl.ds(b * ZR, ZR), pl.ds(256, 64)] = v[:, :64]
        gout[1, pl.ds(b * ZR, ZR), pl.ds(256, 64)] = v[:, 64:]
    v = gath[14].astype(F32)
    gout[2, pl.ds(0, ZR), pl.ds(256, 64)] = v[:, :64]
    gout[2, pl.ds(ZR, ZR), pl.ds(256, 64)] = v[:, 64:]
    for c in started:
        c.wait_send()


def body(activations, norm_gain, norm_bias, spatial_weight, temporal_weight, cotangent):
    vm = pl.BlockSpec(memory_space=pltpu.VMEM)
    hbm = pl.BlockSpec(memory_space=pltpu.HBM)
    V = pltpu.VMEM
    zc = (ZR, 128)
    scratch = [
        V((1, 2, ROWS, COLS, CH), BF16),
        V((1, 2, ROWS, COLS, CH), BF16),
        V((9, CH, CH), BF16),
        V((3, CH, CH), BF16),
        V((CH,), F32),
        V((CH,), F32),
        V((4, 8, CH), F32),
        V((8, HR + 2 * PCOLS, CH), BF16),
        V((8 * FP, CH), BF16),
        V((2, 3, FP, CH), BF16),
        V((2, CUT, CH), BF16),
        V((2, FP - CUT, CH), BF16),
        V((2, 2, FP, CH), BF16),
        V((10 * FP, CH), BF16),
        V((16,) + zc, F32),
        V((4,) + zc, BF16),
        V((4,) + zc, BF16),
        V((4,) + zc, BF16),
        V((3,) + zc, BF16),
        V((4,) + zc, BF16),
        V((4,) + zc, BF16),
        V((4,) + zc, BF16),
        V((3,) + zc, BF16),
        V(zc, F32),
        V(zc, F32),
        V((16,) + zc, BF16),
        V((4, FP, CH), F32),
        V((FP, CH), F32),
        V((2 * FP, CH), F32),
        V((2 * FP, CH), F32),
        V((2 * FP, CH), F32),
        V((2 * FP, CH), F32),
        V((2 * FP, CH), BF16),
        V((2 * FP, CH), BF16),
        pltpu.SemaphoreType.DMA((6,)),
        pltpu.SemaphoreType.DMA((80,)),
        pltpu.SemaphoreType.DMA((80,)),
    ]
    return pl.pallas_call(
        kernel,
        out_shape=(
            jax.ShapeDtypeStruct((1, 2, ROWS, COLS, CH), BF16),
            jax.ShapeDtypeStruct((3, CH, CH), F32),
        ),
        in_specs=[hbm] * 6,
        out_specs=(vm, vm),
        scratch_shapes=scratch,
        compiler_params=pltpu.CompilerParams(
            collective_id=0, has_side_effects=True, vmem_limit_bytes=60 * 2**20
        ),
        name="block",
    )(
        activations,
        norm_gain,
        norm_bias,
        spatial_weight,
        temporal_weight,
        cotangent,
    )


def solution(mesh):
    in_specs = (
        P("dp", "tm", None, None, "mp"),
        P("mp"),
        P("mp"),
        P(None, "mp", "tm"),
        P(None, "tm", "mp"),
        P("dp", "tm", None, None, "mp"),
    )
    out_specs = (P("dp", "tm", None, None, "mp"), P(None, "tm", "mp"))
    return jax.shard_map(body, mesh=mesh, in_specs=in_specs, out_specs=out_specs, check_vma=False)
```

```python
import jax
import jax.numpy as jnp
from jax import lax
from jax.experimental import pallas as pl
from jax.experimental.pallas import tpu as pltpu
from jax.sharding import PartitionSpec as P

MESH = pl.DeviceIdType.MESH
F32, BF16 = jnp.float32, jnp.bfloat16

CH = 320
GROUP = 40
ROWS, COLS, PCOLS = 5, 40, 48
FR = ROWS * COLS
FP = 208
CUT = 112
HR = ROWS * PCOLS
ZR = 160
HZ = ZR // 2
EPS = 1e-05


def dot(a, b, **kw):
    return jnp.dot(a, b, preferred_element_type=F32, **kw)


def kernel(
    act, gain, bias, ws, wt, cot, out, gout,
    actv, cotv, wsv, wtv, gainv, biasv, stats, hid, cotp, part, far_r, far_l, near, spat,
    grad, s1r, s2r, s1l, s2l, r1r, r2r, r1l, r2l, yhs, yhr, gath, hold, mine,
    tpre, tsame, tsend0, tsend1, ysend, yrecv, lsem, ssem, rsem,
):
    dp, tm, mp = lax.axis_index("dp"), lax.axis_index("tm"), lax.axis_index("mp")
    core, yl = lax.rem(tm, 2), lax.div(tm, 2)
    z, yh = lax.div(dp, 2), lax.rem(dp, 2)
    tc = tm + 1 - 2 * core
    ty = lax.rem(tm + 2, 4)
    tyc = lax.rem(tc + 2, 4)

    def zdev(s):
        return {"dp": lax.rem(dp + (2 * s + 32), 32)}

    def xdev(s):
        return {"mp": lax.rem(mp + (s + 4), 4)}

    names = {}

    def rc(name, src, dst, dev):
        i = names.setdefault(name, len(names))
        return pltpu.make_async_remote_copy(
            src_ref=src, dst_ref=dst, send_sem=ssem.at[i], recv_sem=rsem.at[i],
            device_id=dev, device_id_type=MESH,
        )

    started = []

    def send(name, src, dst, dev):
        c = rc(name, src, dst, dev)
        c.start()
        started.append(c)

    def arrived(name, dst, dev):
        rc(name, dst, dst, dev).wait_recv()

    c_act = pltpu.make_async_copy(act, actv, lsem.at[0])
    c_ws = pltpu.make_async_copy(ws, wsv, lsem.at[1])
    c_cot = pltpu.make_async_copy(cot, cotv, lsem.at[2])
    c_wt = pltpu.make_async_copy(wt, wtv, lsem.at[3])
    c_gain = pltpu.make_async_copy(gain, gainv, lsem.at[4])
    c_bias = pltpu.make_async_copy(bias, biasv, lsem.at[5])
    for c in (c_act, c_gain, c_bias, c_cot, c_ws, c_wt):
        c.start()
    yhd = {"dp": dp + 1 - 2 * yh}
    peers = [{"tm": tc}, {"tm": ty}, {"tm": tyc}, xdev(1), xdev(-1)]
    peers += [zdev(1), zdev(-1), zdev(2), zdev(-2), yhd]
    barrier = pltpu.get_barrier_semaphore()
    for p in peers:
        pl.semaphore_signal(barrier, inc=1, device_id=p, device_id_type=MESH)

    zrows = jnp.zeros((8, PCOLS, CH), BF16)
    hid[:, pl.ds(0, PCOLS), :] = zrows
    hid[:, pl.ds(PCOLS + HR, PCOLS), :] = zrows
    spat[pl.ds(0, FP), :] = jnp.zeros((FP, CH), BF16)
    spat[pl.ds(9 * FP, FP), :] = jnp.zeros((FP, CH), BF16)
    grad[15] = jnp.zeros((ZR, 128), F32)

    c_act.wait()
    x = actv[...].astype(F32).reshape(2 * FR, CH)
    ssum = jnp.sum(x, axis=0, keepdims=True)
    cen = x - ssum * (1.0 / (2 * FR))
    m2 = jnp.sum(cen * cen, axis=0, keepdims=True)
    r8 = lax.broadcasted_iota(jnp.int32, (8, CH), 0)
    stats[tm] = jnp.where(r8 == 0, ssum, jnp.where(r8 == 1, m2, 0.0))

    pl.semaphore_wait(barrier, len(peers))
    send("st_c", stats.at[tm], stats.at[tm], {"tm": tc})
    send("st_y", stats.at[tm], stats.at[tm], {"tm": ty})
    send("st_yc", stats.at[tm], stats.at[tm], {"tm": tyc})

    gi = lax.broadcasted_iota(jnp.int32, (CH, CH), 0)
    gj = lax.broadcasted_iota(jnp.int32, (CH, CH), 1)
    same = (((gi * 1639) >> 16) == ((gj * 1639) >> 16)).astype(F32)

    c_cot.wait()
    zpad = jnp.zeros((FP - FR, CH), F32)
    for i in range(2):
        cf = cotv[0, i].astype(F32).reshape(FR, CH)
        cotp[pl.ds(pl.multiple_of((2 * tm + i) * FP, FP), FP), :] = jnp.concatenate(
            [cf, zpad], axis=0
        ).astype(BF16)

    arrived("st_c", stats.at[tc], {"tm": tc})
    arrived("st_y", stats.at[ty], {"tm": ty})
    arrived("st_yc", stats.at[tyc], {"tm": tyc})
    st = [stats[i] for i in range(4)]
    total = st[0] + st[1] + st[2] + st[3]
    hi = lax.Precision.HIGHEST
    avg = dot(total, same, precision=hi)[0:1] * (1.0 / (8 * FR * GROUP))
    m2all = total[1:2]
    for i in range(4):
        dm = st[i][0:1] * (1.0 / (2 * FR)) - avg
        m2all = m2all + (2.0 * FR) * dm * dm
    m2all = jnp.broadcast_to(m2all, (8, CH))
    var = dot(m2all, same, precision=hi)[0:1] * (1.0 / (8 * FR * GROUP))
    c_gain.wait()
    c_bias.wait()
    inv = lax.rsqrt(var + EPS) * gainv[...].reshape(1, CH)
    bia = biasv[...].reshape(1, CH)

    for i in range(2):
        xf = actv[0, i].astype(F32).reshape(FR, CH)
        nf = (xf - avg) * inv + bia
        hf = nf * (1.0 / (1.0 + jnp.exp(-nf)))
        hf = jnp.concatenate(
            [hf.reshape(ROWS, COLS, CH), jnp.zeros((ROWS, PCOLS - COLS, CH), F32)], axis=1
        )
        hid[2 * tm + i, pl.ds(PCOLS, HR), :] = hf.reshape(HR, CH).astype(BF16)
        own = hid.at[2 * tm + i, pl.ds(PCOLS, HR), :]
        send(f"hy{i}", own, own, {"tm": ty})
        send(f"hc{i}", own, own, {"tm": tc})

    def cframes(t):
        return cotp.at[pl.ds(pl.multiple_of(2 * t * FP, FP), 2 * FP), :]

    def hframe(f):
        return hid.at[f, pl.ds(PCOLS, HR), :]

    def relay_hidden(i):
        return rc(f"hr{i}", hframe(2 * ty + i), hframe(2 * ty + i), {"tm": tc})

    def conv(f):
        acc = []
        for b in range(3):
            v = dot(hid[f, pl.ds(0, HR), :], wsv[b])
            for a in (1, 2):
                v = v + dot(hid[f, pl.ds(PCOLS * a, HR), :], wsv[3 * a + b])
            acc.append(v)
        o = acc[1] + pltpu.roll(acc[0], 1, 0) + pltpu.roll(acc[2], HR - 1, 0)
        o = o.reshape(ROWS, PCOLS, CH)[:, :COLS, :].reshape(FR, CH)
        return jnp.concatenate([o, zpad], axis=0)

    def sframe(f):
        return pl.ds(pl.multiple_of((f + 1) * FP, FP), FP)

    top, low = pl.ds(0, CUT), pl.ds(CUT, FP - CUT)

    def far(h):
        return (
            rc(f"fr{h}", part.at[h, 0, top], far_r.at[h], xdev(1)),
            rc(f"fl{h}", part.at[h, 0, low], far_l.at[h], xdev(-1)),
        )

    def near_early(h):
        return (
            rc(f"nrl{h}", part.at[h, 1, low], near.at[h, 0, low], xdev(1)),
            rc(f"nlt{h}", part.at[h, 2, top], near.at[h, 1, top], xdev(-1)),
        )

    def gathers(h, base):
        f = base + mp
        t, b = spart(f, 0, CUT), spart(f, CUT, FP - CUT)
        return (
            rc(f"grt{h}", t, t, xdev(1)),
            rc(f"glb{h}", b, b, xdev(-1)),
            rc(f"grb{h}", b, b, xdev(1)),
            rc(f"glt{h}", t, t, xdev(-1)),
        )

    def half_convs(h, base, hook):
        def step(j, _):
            q, r = lax.div(j, 2), lax.rem(j, 2)
            off = 2 + q - r - 2 * q * r
            hold[j] = conv(base + lax.rem(mp + off, 4))

            @pl.when(j == 0)
            def _():
                part[h, 0] = hold[0].astype(BF16)
                for c in far(h):
                    c.start()

            @pl.when(j == 1)
            def _():
                part[h, 1, low] = hold[1, low].astype(BF16)
                near_early(h)[0].start()

            @pl.when(j == 2)
            def _():
                part[h, 2, top] = hold[2, top].astype(BF16)
                near_early(h)[1].start()

            hook(j)
            return 0

        lax.fori_loop(0, 4, step, 0)
        started.extend(far(h))
        started.extend(near_early(h))

    def half_near(h):
        arrived(f"fr{h}", far_r.at[h], xdev(-1))
        part[h, 1, top] = (hold[1, top] + far_r[h].astype(F32)).astype(BF16)
        send(f"nrt{h}", part.at[h, 1, top], near.at[h, 0, top], xdev(1))
        arrived(f"fl{h}", far_l.at[h], xdev(1))
        part[h, 2, low] = (hold[2, low] + far_l[h].astype(F32)).astype(BF16)
        send(f"nll{h}", part.at[h, 2, low], near.at[h, 1, low], xdev(-1))
        mine[...] = hold[3]

    def half_sum(h, base):
        arrived(f"nrl{h}", near.at[h, 0, low], xdev(-1))
        arrived(f"nlt{h}", near.at[h, 1, top], xdev(1))
        arrived(f"nrt{h}", near.at[h, 0, top], xdev(-1))
        arrived(f"nll{h}", near.at[h, 1, low], xdev(1))
        whole = mine[...] + near[h, 0].astype(F32) + near[h, 1].astype(F32)
        spat[sframe(base + mp), :] = whole.astype(BF16)
        for c in gathers(h, base):
            c.start()

    def spart(f, lo, n):
        return spat.at[pl.ds(pl.multiple_of((f + 1) * FP + lo, 16), n), :]

    def forwards(h, base):
        lf, rf = base + lax.rem(mp + 3, 4), base + lax.rem(mp + 1, 4)
        return (
            rc(f"wr{h}", spart(lf, 0, CUT), spart(lf, 0, CUT), xdev(1)),
            rc(f"wl{h}", spart(rf, CUT, FP - CUT), spart(rf, CUT, FP - CUT), xdev(-1)),
        )

    def half_forward(h, base):
        lf, rf = base + lax.rem(mp + 3, 4), base + lax.rem(mp + 1, 4)
        to_r, to_l = forwards(h, base)
        arrived(f"grt{h}", spart(lf, 0, CUT), xdev(-1))
        to_r.start()
        arrived(f"glb{h}", spart(rf, CUT, FP - CUT), xdev(1))
        to_l.start()

    def half_done(h, base):
        lf, rf = base + lax.rem(mp + 3, 4), base + lax.rem(mp + 1, 4)
        ff = base + lax.rem(mp + 2, 4)
        arrived(f"grb{h}", spart(lf, CUT, FP - CUT), xdev(-1))
        arrived(f"glt{h}", spart(rf, 0, CUT), xdev(1))
        arrived(f"wr{h}", spart(ff, 0, CUT), xdev(-1))
        arrived(f"wl{h}", spart(ff, CUT, FP - CUT), xdev(1))

    base0, base1 = 4 * yl, 4 * (1 - yl)
    c_ws.wait()
    for i in range(2):
        arrived(f"hc{i}", hframe(2 * tc + i), {"tm": tc})

    half_convs(0, base0, lambda j: None)
    half_near(0)
    for i in range(2):
        arrived(f"hy{i}", hframe(2 * ty + i), {"tm": ty})
        c = relay_hidden(i)
        c.start()
        started.append(c)
    send("cy", cframes(tm), cframes(tm), {"tm": ty})
    for i in range(2):
        arrived(f"hr{i}", hframe(2 * tyc + i), {"tm": tc})

    def between(j):
        @pl.when(j == 1)
        def _():
            half_sum(0, base0)

    half_convs(1, base1, between)
    started.extend(gathers(0, base0))
    half_near(1)
    send("cc", cframes(tm), cframes(tm), {"tm": tc})
    half_forward(0, base0)
    started.extend(forwards(0, base0))
    half_sum(1, base1)
    started.extend(gathers(1, base1))
    arrived("cc", cframes(tc), {"tm": tc})
    arrived("cy", cframes(ty), {"tm": ty})
    send("cr", cframes(ty), cframes(ty), {"tm": tc})
    half_forward(1, base1)
    started.extend(forwards(1, base1))
    arrived("cr", cframes(tyc), {"tm": tc})
    half_done(0, base0)
    half_done(1, base1)
    c_wt.wait()

    tails = []
    for k in range(3):
        g = lax.dot_general(
            spat[pl.ds(k * FP, 8 * FP), :], cotp[...], (((0,), (0,)), ((), ())),
            preferred_element_type=F32,
        )
        for a in range(2):
            grad[pl.ds(4 * k + 2 * a, 2)] = g[:, 128 * a : 128 * a + 128].reshape(2, ZR, 128)
        tails.append(g[:, 256:])
    grad[pl.ds(12, 2)] = jnp.concatenate(tails[:2], axis=1).reshape(2, ZR, 128)
    grad[14] = jnp.concatenate([tails[2][:ZR], tails[2][ZR:]], axis=1)

    order = (8, 7, -7, 6, -6, 5, -5, 4, -4, 3, -3, 2, -2, 1, -1, 0)
    bounds = (0, 3, 7, 11, 15, 16)
    mine_z = pl.ds(pl.multiple_of(yh * HZ, HZ), HZ)
    other_z = pl.ds(pl.multiple_of((1 - yh) * HZ, HZ), HZ)

    def at_z(s):
        return lax.rem(z + (s + 32), 16)

    def group(g):
        return pl.ds(bounds[g], bounds[g + 1] - bounds[g])

    for g in range(5):
        for p in range(bounds[g], bounds[g + 1]):
            yhs[p] = grad[at_z(order[p]), other_z, :].astype(BF16)
        send(f"yg{g}", yhs.at[group(g)], yhr.at[group(g)], yhd)
    got = set()

    def own(s):
        p = order.index(s)
        g = max(i for i in range(5) if bounds[i] <= p)
        if g not in got:
            got.add(g)
            arrived(f"yg{g}", yhr.at[group(g)], yhd)
        return grad[at_z(s), mine_z, :] + yhr[p].astype(F32)

    def one_hop(i):
        s1r[i] = own(2 * i + 1).astype(BF16)
        s1l[i] = own(-2 * i - 1).astype(BF16)
        send(f"or{i}", s1r.at[i], r1r.at[i], zdev(1))
        send(f"ol{i}", s1l.at[i], r1l.at[i], zdev(-1))

    s2r[0] = own(8).astype(BF16)
    send("zr0", s2r.at[0], r2r.at[0], zdev(2))
    one_hop(3)

    def temporal(t):
        r0 = pl.multiple_of(2 * t * FP, FP)
        v = dot(spat[pl.ds(r0, 2 * FP), :], wtv[0])
        for k in (1, 2):
            v = v + dot(spat[pl.ds(pl.multiple_of(r0 + k * FP, FP), 2 * FP), :], wtv[k])
        return v

    tsend0[...] = temporal(tyc)
    send("tp", tsend0, tpre, {"tm": tc})

    def chain_r(i):
        arrived(f"or{4 - i}", r1r.at[4 - i], zdev(-1))
        arrived(f"zr{i - 1}", r2r.at[i - 1], zdev(-2))
        v = own(8 - 2 * i) + r1r[4 - i].astype(F32) + r2r[i - 1].astype(F32)
        if i < 4:
            s2r[i] = v.astype(BF16)
            send(f"zr{i}", s2r.at[i], r2r.at[i], zdev(2))
        return v

    def chain_l(i):
        arrived(f"ol{3 - i}", r1l.at[3 - i], zdev(1))
        v = r1l[3 - i].astype(F32)
        if i > 0:
            arrived(f"zl{i - 1}", r2l.at[i - 1], zdev(2))
            v = v + r2l[i - 1].astype(F32)
        if i < 3:
            s2l[i] = (own(-6 + 2 * i) + v).astype(BF16)
            send(f"zl{i}", s2l.at[i], r2l.at[i], zdev(-2))
        return v

    chain_l(0)
    chain_r(1)
    one_hop(2)
    tsend1[...] = temporal(tc)
    send("ts", tsend1, tsame, {"tm": tc})
    chain_l(1)
    chain_r(2)
    one_hop(1)
    tacc = temporal(ty)
    arrived("tp", tpre, {"tm": tc})
    ysend[...] = (tacc + tpre[...]).astype(BF16)
    send("ty", ysend, yrecv, {"tm": ty})
    chain_l(2)
    chain_r(3)
    one_hop(0)
    tsend_own = temporal(tm)
    arrived("ts", tsame, {"tm": tc})
    tsame[...] = tsame[...] + tsend_own
    gath[z, mine_z, :] = ((chain_l(3) + chain_r(4)) * (1.0 / 32.0)).astype(BF16)

    def slot(s):
        return gath.at[at_z(s), mine_z, :]

    def hand(s):
        send(f"yf{s}", slot(s), slot(s), yhd)

    send("ar0", slot(0), slot(0), zdev(2))
    send("al0", slot(0), slot(0), zdev(-2))
    send("br0", slot(0), slot(0), zdev(1))
    send("bl0", slot(0), slot(0), zdev(-1))
    hand(0)
    arrived("ty", yrecv, {"tm": ty})
    res = tsame[...] + yrecv[...].astype(F32)
    for i in range(2):
        out[0, i] = res[i * FP : i * FP + FR].reshape(ROWS, COLS, CH).astype(BF16)
    for i in (1, 2, 3):
        arrived(f"ar{i - 1}", slot(-2 * i), zdev(-2))
        send(f"ar{i}", slot(-2 * i), slot(-2 * i), zdev(2))
        arrived(f"al{i - 1}", slot(2 * i), zdev(2))
        if i < 3:
            send(f"al{i}", slot(2 * i), slot(2 * i), zdev(-2))
        send(f"br{i}", slot(-2 * i), slot(-2 * i), zdev(1))
        send(f"bl{i}", slot(2 * i), slot(2 * i), zdev(-1))
        hand(-2 * i)
        hand(2 * i)
        arrived(f"br{i - 1}", slot(1 - 2 * i), zdev(-1))
        hand(1 - 2 * i)
        arrived(f"bl{i - 1}", slot(2 * i - 1), zdev(1))
        hand(2 * i - 1)
    arrived("ar3", slot(-8), zdev(-2))
    hand(-8)
    arrived("br3", slot(-7), zdev(-1))
    hand(-7)
    arrived("bl3", slot(7), zdev(1))
    hand(7)
    for s in (0, -2, 2, -1, 1, -4, 4, -3, 3, -6, 6, -5, 5, -8, -7, 7):
        arrived(f"yf{s}", gath.at[at_z(s), other_z, :], yhd)
    for j in range(12):
        k, a, b = j // 4, j // 2 % 2, j % 2
        gout[k, pl.ds(b * ZR, ZR), pl.ds(128 * a, 128)] = gath[j].astype(F32)
    for b in range(2):
        v = gath[12 + b].astype(F32)
        gout[0, pl.ds(b * ZR, ZR), pl.ds(256, 64)] = v[:, :64]
        gout[1, pl.ds(b * ZR, ZR), pl.ds(256, 64)] = v[:, 64:]
    v = gath[14].astype(F32)
    gout[2, pl.ds(0, ZR), pl.ds(256, 64)] = v[:, :64]
    gout[2, pl.ds(ZR, ZR), pl.ds(256, 64)] = v[:, 64:]
    for c in started:
        c.wait_send()


def body(activations, norm_gain, norm_bias, spatial_weight, temporal_weight, cotangent):
    vm = pl.BlockSpec(memory_space=pltpu.VMEM)
    hbm = pl.BlockSpec(memory_space=pltpu.HBM)
    V = pltpu.VMEM
    zc = (HZ, 128)
    scratch = [
        V((1, 2, ROWS, COLS, CH), BF16),
        V((1, 2, ROWS, COLS, CH), BF16),
        V((9, CH, CH), BF16),
        V((3, CH, CH), BF16),
        V((CH,), F32),
        V((CH,), F32),
        V((4, 8, CH), F32),
        V((8, HR + 2 * PCOLS, CH), BF16),
        V((8 * FP, CH), BF16),
        V((2, 3, FP, CH), BF16),
        V((2, CUT, CH), BF16),
        V((2, FP - CUT, CH), BF16),
        V((2, 2, FP, CH), BF16),
        V((10 * FP, CH), BF16),
        V((16, ZR, 128), F32),
        V((4,) + zc, BF16),
        V((4,) + zc, BF16),
        V((4,) + zc, BF16),
        V((3,) + zc, BF16),
        V((4,) + zc, BF16),
        V((4,) + zc, BF16),
        V((4,) + zc, BF16),
        V((3,) + zc, BF16),
        V((16,) + zc, BF16),
        V((16,) + zc, BF16),
        V((16, ZR, 128), BF16),
        V((4, FP, CH), F32),
        V((FP, CH), F32),
        V((2 * FP, CH), F32),
        V((2 * FP, CH), F32),
        V((2 * FP, CH), F32),
        V((2 * FP, CH), F32),
        V((2 * FP, CH), BF16),
        V((2 * FP, CH), BF16),
        pltpu.SemaphoreType.DMA((6,)),
        pltpu.SemaphoreType.DMA((112,)),
        pltpu.SemaphoreType.DMA((112,)),
    ]
    return pl.pallas_call(
        kernel,
        out_shape=(
            jax.ShapeDtypeStruct((1, 2, ROWS, COLS, CH), BF16),
            jax.ShapeDtypeStruct((3, CH, CH), F32),
        ),
        in_specs=[hbm] * 6,
        out_specs=(vm, vm),
        scratch_shapes=scratch,
        compiler_params=pltpu.CompilerParams(
            collective_id=0, has_side_effects=True, vmem_limit_bytes=48 * 2**20
        ),
        name="block",
    )(
        *(
            pltpu.with_memory_space_constraint(v, pltpu.HBM)
            for v in (
                activations, norm_gain, norm_bias, spatial_weight, temporal_weight, cotangent,
            )
        )
    )


def solution(mesh):
    in_specs = (
        P("dp", "tm", None, None, "mp"),
        P("mp"),
        P("mp"),
        P(None, "mp", "tm"),
        P(None, "tm", "mp"),
        P("dp", "tm", None, None, "mp"),
    )
    out_specs = (P("dp", "tm", None, None, "mp"), P(None, "tm", "mp"))
    return jax.shard_map(body, mesh=mesh, in_specs=in_specs, out_specs=out_specs, check_vma=False)
```

```python
import jax
import jax.numpy as jnp
from jax import lax
from jax.experimental import pallas as pl
from jax.experimental.pallas import tpu as pltpu
from jax.sharding import PartitionSpec as P

MESH = pl.DeviceIdType.MESH
F32, BF16 = jnp.float32, jnp.bfloat16

CH = 320
GROUP = 40
ROWS, COLS, PCOLS = 5, 40, 48
FR = ROWS * COLS
FP = 208
CUT = 112
HR = ROWS * PCOLS
ZR = 160
HZ = ZR // 2
EPS = 1e-05


def dot(a, b, **kw):
    return jnp.dot(a, b, preferred_element_type=F32, **kw)


def kernel(
    act, gain, bias, ws, wt, cot, out, gout,
    actv, cotv, wsv, wtv, gainv, biasv, stats, hid, cotp, part, far_r, far_l, near, spat,
    grad, sr, sl, rr, rl, yhs, yhr, gath, hold, mine,
    tpre, tsame, tsend0, tsend1, ysend, yrecv, lsem, ssem, rsem,
):
    dp, tm, mp = lax.axis_index("dp"), lax.axis_index("tm"), lax.axis_index("mp")
    core, yl = lax.rem(tm, 2), lax.div(tm, 2)
    z, yh = lax.div(dp, 2), lax.rem(dp, 2)
    tc = tm + 1 - 2 * core
    ty = lax.rem(tm + 2, 4)
    tyc = lax.rem(tc + 2, 4)

    def zdev(s):
        return {"dp": lax.rem(dp + (2 * s + 32), 32)}

    def xdev(s):
        return {"mp": lax.rem(mp + (s + 4), 4)}

    names = {}

    def rc(name, src, dst, dev):
        i = names.setdefault(name, len(names))
        return pltpu.make_async_remote_copy(
            src_ref=src, dst_ref=dst, send_sem=ssem.at[i], recv_sem=rsem.at[i],
            device_id=dev, device_id_type=MESH,
        )

    started = []

    def send(name, src, dst, dev):
        c = rc(name, src, dst, dev)
        c.start()
        started.append(c)

    def arrived(name, dst, dev):
        rc(name, dst, dst, dev).wait_recv()

    c_act = pltpu.make_async_copy(act, actv, lsem.at[0])
    c_ws = pltpu.make_async_copy(ws, wsv, lsem.at[1])
    c_cot = pltpu.make_async_copy(cot, cotv, lsem.at[2])
    c_wt = pltpu.make_async_copy(wt, wtv, lsem.at[3])
    c_gain = pltpu.make_async_copy(gain, gainv, lsem.at[4])
    c_bias = pltpu.make_async_copy(bias, biasv, lsem.at[5])
    for c in (c_act, c_gain, c_bias, c_cot, c_ws, c_wt):
        c.start()
    yhd = {"dp": dp + 1 - 2 * yh}
    peers = [{"tm": tc}, {"tm": ty}, {"tm": tyc}, xdev(1), xdev(-1)]
    peers += [zdev(h) for h in (1, 2, 3, 4, -1, -2, -3, -4)] + [yhd]
    barrier = pltpu.get_barrier_semaphore()
    for p in peers:
        pl.semaphore_signal(barrier, inc=1, device_id=p, device_id_type=MESH)

    zrows = jnp.zeros((8, PCOLS, CH), BF16)
    hid[:, pl.ds(0, PCOLS), :] = zrows
    hid[:, pl.ds(PCOLS + HR, PCOLS), :] = zrows
    spat[pl.ds(0, FP), :] = jnp.zeros((FP, CH), BF16)
    spat[pl.ds(9 * FP, FP), :] = jnp.zeros((FP, CH), BF16)
    grad[15] = jnp.zeros((ZR, 128), F32)

    c_act.wait()
    x = actv[...].astype(F32).reshape(2 * FR, CH)
    ssum = jnp.sum(x, axis=0, keepdims=True)
    cen = x - ssum * (1.0 / (2 * FR))
    m2 = jnp.sum(cen * cen, axis=0, keepdims=True)
    r8 = lax.broadcasted_iota(jnp.int32, (8, CH), 0)
    stats[tm] = jnp.where(r8 == 0, ssum, jnp.where(r8 == 1, m2, 0.0))

    pl.semaphore_wait(barrier, len(peers))
    send("st_c", stats.at[tm], stats.at[tm], {"tm": tc})
    send("st_y", stats.at[tm], stats.at[tm], {"tm": ty})
    send("st_yc", stats.at[tm], stats.at[tm], {"tm": tyc})

    gi = lax.broadcasted_iota(jnp.int32, (CH, CH), 0)
    gj = lax.broadcasted_iota(jnp.int32, (CH, CH), 1)
    same = (((gi * 1639) >> 16) == ((gj * 1639) >> 16)).astype(F32)

    c_cot.wait()
    zpad = jnp.zeros((FP - FR, CH), F32)
    for i in range(2):
        cf = cotv[0, i].astype(F32).reshape(FR, CH)
        cotp[pl.ds(pl.multiple_of((2 * tm + i) * FP, FP), FP), :] = jnp.concatenate(
            [cf, zpad], axis=0
        ).astype(BF16)

    arrived("st_c", stats.at[tc], {"tm": tc})
    arrived("st_y", stats.at[ty], {"tm": ty})
    arrived("st_yc", stats.at[tyc], {"tm": tyc})
    st = [stats[i] for i in range(4)]
    total = st[0] + st[1] + st[2] + st[3]
    hi = lax.Precision.HIGHEST
    avg = dot(total, same, precision=hi)[0:1] * (1.0 / (8 * FR * GROUP))
    m2all = total[1:2]
    for i in range(4):
        dm = st[i][0:1] * (1.0 / (2 * FR)) - avg
        m2all = m2all + (2.0 * FR) * dm * dm
    m2all = jnp.broadcast_to(m2all, (8, CH))
    var = dot(m2all, same, precision=hi)[0:1] * (1.0 / (8 * FR * GROUP))
    c_gain.wait()
    c_bias.wait()
    inv = lax.rsqrt(var + EPS) * gainv[...].reshape(1, CH)
    bia = biasv[...].reshape(1, CH)

    for i in range(2):
        xf = actv[0, i].astype(F32).reshape(FR, CH)
        nf = (xf - avg) * inv + bia
        hf = nf * (1.0 / (1.0 + jnp.exp(-nf)))
        hf = jnp.concatenate(
            [hf.reshape(ROWS, COLS, CH), jnp.zeros((ROWS, PCOLS - COLS, CH), F32)], axis=1
        )
        hid[2 * tm + i, pl.ds(PCOLS, HR), :] = hf.reshape(HR, CH).astype(BF16)
        own = hid.at[2 * tm + i, pl.ds(PCOLS, HR), :]
        send(f"hy{i}", own, own, {"tm": ty})
        send(f"hc{i}", own, own, {"tm": tc})

    def cframes(t):
        return cotp.at[pl.ds(pl.multiple_of(2 * t * FP, FP), 2 * FP), :]

    def hframe(f):
        return hid.at[f, pl.ds(PCOLS, HR), :]

    def relay_hidden(i):
        return rc(f"hr{i}", hframe(2 * ty + i), hframe(2 * ty + i), {"tm": tc})

    def conv(f):
        acc = []
        for b in range(3):
            v = dot(hid[f, pl.ds(0, HR), :], wsv[b])
            for a in (1, 2):
                v = v + dot(hid[f, pl.ds(PCOLS * a, HR), :], wsv[3 * a + b])
            acc.append(v)
        o = acc[1] + pltpu.roll(acc[0], 1, 0) + pltpu.roll(acc[2], HR - 1, 0)
        o = o.reshape(ROWS, PCOLS, CH)[:, :COLS, :].reshape(FR, CH)
        return jnp.concatenate([o, zpad], axis=0)

    def sframe(f):
        return pl.ds(pl.multiple_of((f + 1) * FP, FP), FP)

    top, low = pl.ds(0, CUT), pl.ds(CUT, FP - CUT)

    def far(h):
        return (
            rc(f"fr{h}", part.at[h, 0, top], far_r.at[h], xdev(1)),
            rc(f"fl{h}", part.at[h, 0, low], far_l.at[h], xdev(-1)),
        )

    def near_early(h):
        return (
            rc(f"nrl{h}", part.at[h, 1, low], near.at[h, 0, low], xdev(1)),
            rc(f"nlt{h}", part.at[h, 2, top], near.at[h, 1, top], xdev(-1)),
        )

    def gathers(h, base):
        f = base + mp
        t, b = spart(f, 0, CUT), spart(f, CUT, FP - CUT)
        return (
            rc(f"grt{h}", t, t, xdev(1)),
            rc(f"glb{h}", b, b, xdev(-1)),
            rc(f"grb{h}", b, b, xdev(1)),
            rc(f"glt{h}", t, t, xdev(-1)),
        )

    def half_convs(h, base, hook):
        def step(j, _):
            q, r = lax.div(j, 2), lax.rem(j, 2)
            off = 2 + q - r - 2 * q * r
            hold[j] = conv(base + lax.rem(mp + off, 4))

            @pl.when(j == 0)
            def _():
                part[h, 0] = hold[0].astype(BF16)
                for c in far(h):
                    c.start()

            @pl.when(j == 1)
            def _():
                part[h, 1, low] = hold[1, low].astype(BF16)
                near_early(h)[0].start()

            @pl.when(j == 2)
            def _():
                part[h, 2, top] = hold[2, top].astype(BF16)
                near_early(h)[1].start()

            hook(j)
            return 0

        lax.fori_loop(0, 4, step, 0)
        started.extend(far(h))
        started.extend(near_early(h))

    def half_near(h):
        arrived(f"fr{h}", far_r.at[h], xdev(-1))
        part[h, 1, top] = (hold[1, top] + far_r[h].astype(F32)).astype(BF16)
        send(f"nrt{h}", part.at[h, 1, top], near.at[h, 0, top], xdev(1))
        arrived(f"fl{h}", far_l.at[h], xdev(1))
        part[h, 2, low] = (hold[2, low] + far_l[h].astype(F32)).astype(BF16)
        send(f"nll{h}", part.at[h, 2, low], near.at[h, 1, low], xdev(-1))
        mine[...] = hold[3]

    def half_sum(h, base):
        arrived(f"nrl{h}", near.at[h, 0, low], xdev(-1))
        arrived(f"nlt{h}", near.at[h, 1, top], xdev(1))
        arrived(f"nrt{h}", near.at[h, 0, top], xdev(-1))
        arrived(f"nll{h}", near.at[h, 1, low], xdev(1))
        whole = mine[...] + near[h, 0].astype(F32) + near[h, 1].astype(F32)
        spat[sframe(base + mp), :] = whole.astype(BF16)
        for c in gathers(h, base):
            c.start()

    def spart(f, lo, n):
        return spat.at[pl.ds(pl.multiple_of((f + 1) * FP + lo, 16), n), :]

    def forwards(h, base):
        lf, rf = base + lax.rem(mp + 3, 4), base + lax.rem(mp + 1, 4)
        return (
            rc(f"wr{h}", spart(lf, 0, CUT), spart(lf, 0, CUT), xdev(1)),
            rc(f"wl{h}", spart(rf, CUT, FP - CUT), spart(rf, CUT, FP - CUT), xdev(-1)),
        )

    def half_forward(h, base):
        lf, rf = base + lax.rem(mp + 3, 4), base + lax.rem(mp + 1, 4)
        to_r, to_l = forwards(h, base)
        arrived(f"grt{h}", spart(lf, 0, CUT), xdev(-1))
        to_r.start()
        arrived(f"glb{h}", spart(rf, CUT, FP - CUT), xdev(1))
        to_l.start()

    def half_done(h, base):
        lf, rf = base + lax.rem(mp + 3, 4), base + lax.rem(mp + 1, 4)
        ff = base + lax.rem(mp + 2, 4)
        arrived(f"grb{h}", spart(lf, CUT, FP - CUT), xdev(-1))
        arrived(f"glt{h}", spart(rf, 0, CUT), xdev(1))
        arrived(f"wr{h}", spart(ff, 0, CUT), xdev(-1))
        arrived(f"wl{h}", spart(ff, CUT, FP - CUT), xdev(1))

    base0, base1 = 4 * yl, 4 * (1 - yl)
    c_ws.wait()
    for i in range(2):
        arrived(f"hc{i}", hframe(2 * tc + i), {"tm": tc})

    half_convs(0, base0, lambda j: None)
    half_near(0)
    for i in range(2):
        arrived(f"hy{i}", hframe(2 * ty + i), {"tm": ty})
        c = relay_hidden(i)
        c.start()
        started.append(c)
    send("cy", cframes(tm), cframes(tm), {"tm": ty})
    for i in range(2):
        arrived(f"hr{i}", hframe(2 * tyc + i), {"tm": tc})

    def between(j):
        @pl.when(j == 1)
        def _():
            half_sum(0, base0)

    half_convs(1, base1, between)
    started.extend(gathers(0, base0))
    half_near(1)
    send("cc", cframes(tm), cframes(tm), {"tm": tc})
    half_forward(0, base0)
    started.extend(forwards(0, base0))
    half_sum(1, base1)
    started.extend(gathers(1, base1))
    arrived("cc", cframes(tc), {"tm": tc})
    arrived("cy", cframes(ty), {"tm": ty})
    send("cr", cframes(ty), cframes(ty), {"tm": tc})
    half_forward(1, base1)
    started.extend(forwards(1, base1))
    arrived("cr", cframes(tyc), {"tm": tc})
    half_done(0, base0)
    half_done(1, base1)
    c_wt.wait()

    tails = []
    for k in range(3):
        g = lax.dot_general(
            spat[pl.ds(k * FP, 8 * FP), :], cotp[...], (((0,), (0,)), ((), ())),
            preferred_element_type=F32,
        )
        for a in range(2):
            grad[pl.ds(4 * k + 2 * a, 2)] = g[:, 128 * a : 128 * a + 128].reshape(2, ZR, 128)
        tails.append(g[:, 256:])
    grad[pl.ds(12, 2)] = jnp.concatenate(tails[:2], axis=1).reshape(2, ZR, 128)
    grad[14] = jnp.concatenate([tails[2][:ZR], tails[2][ZR:]], axis=1)

    order = (8, 7, -7, 6, -6, 5, -5, 4, -4, 3, -3, 2, -2, 1, -1, 0)
    bounds = (0, 3, 7, 11, 15, 16)
    mine_z = pl.ds(pl.multiple_of(yh * HZ, HZ), HZ)
    other_z = pl.ds(pl.multiple_of((1 - yh) * HZ, HZ), HZ)

    def at_z(s):
        return lax.rem(z + (s + 32), 16)

    def group(g):
        return pl.ds(bounds[g], bounds[g + 1] - bounds[g])

    def send_group(g):
        for p in range(bounds[g], bounds[g + 1]):
            yhs[p] = grad[at_z(order[p]), other_z, :].astype(BF16)
        send(f"yg{g}", yhs.at[group(g)], yhr.at[group(g)], yhd)

    send_group(0)
    send_group(1)
    got = set()

    def own(s):
        p = order.index(s)
        g = max(i for i in range(5) if bounds[i] <= p)
        if g not in got:
            got.add(g)
            arrived(f"yg{g}", yhr.at[group(g)], yhd)
            if g < 3:
                send_group(g + 2)
        return grad[at_z(s), mine_z, :] + yhr[p].astype(F32)

    ways = ((1, sr, rr), (-1, sl, rl))

    def hops(i):
        return i - 4 if i > 4 else i

    def terms(*far_to_near):
        for i in far_to_near:
            for d, snd, rcv in ways[: 1 if i == 8 else 2]:
                snd[i - 1] = own(d * i).astype(BF16)
                send(f"z{d}_{i}", snd.at[i - 1], rcv.at[i - 1], zdev(d * hops(i)))

    def incoming(d, rcv, steps):
        v = None
        for i in steps:
            if d * i != -8:
                arrived(f"z{d}_{i}", rcv.at[i - 1], zdev(-d * hops(i)))
                t = rcv[i - 1].astype(F32)
                v = t if v is None else v + t
        return v

    def temporal(t):
        r0 = pl.multiple_of(2 * t * FP, FP)
        v = dot(spat[pl.ds(r0, 2 * FP), :], wtv[0])
        for k in (1, 2):
            v = v + dot(spat[pl.ds(pl.multiple_of(r0 + k * FP, FP), 2 * FP), :], wtv[k])
        return v

    tsend0[...] = temporal(tyc)
    send("tp", tsend0, tpre, {"tm": tc})
    terms(8, 7, 6, 5)
    tsend1[...] = temporal(tc)
    send("ts", tsend1, tsame, {"tm": tc})
    terms(3, 2, 1)
    for d, snd, rcv in ways:
        snd[3] = (own(4 * d) + incoming(d, rcv, (5, 6, 7, 8))).astype(BF16)
        send(f"z{d}_4", snd.at[3], rcv.at[3], zdev(4 * d))
    tacc = temporal(ty)
    arrived("tp", tpre, {"tm": tc})
    ysend[...] = (tacc + tpre[...]).astype(BF16)
    send("ty", ysend, yrecv, {"tm": ty})
    tsend_own = temporal(tm)
    arrived("ts", tsame, {"tm": tc})
    tsame[...] = tsame[...] + tsend_own
    zsum = own(0)
    for d, snd, rcv in ways:
        zsum = zsum + incoming(d, rcv, (1, 2, 3, 4))
    gath[z, mine_z, :] = (zsum * (1.0 / 32.0)).astype(BF16)

    def slot(s):
        return gath.at[at_z(s), mine_z, :]

    def hand(s):
        send(f"yf{s}", slot(s), slot(s), yhd)

    for h in (4, 3, 2, 1):
        for d in (1, -1):
            send(f"a{d}_{h}", slot(0), slot(0), zdev(d * h))
    hand(0)
    for h in (1, 2, 3):
        for d in (1, -1):
            arrived(f"a{d}_{h}", slot(-d * h), zdev(-d * h))
            hand(-d * h)
    for d in (1, -1):
        arrived(f"a{d}_4", slot(-4 * d), zdev(-4 * d))
        for h in (4, 3, 2, 1):
            if d * h != -4:
                send(f"b{d}_{h}", slot(-4 * d), slot(-4 * d), zdev(d * h))
    for d in (1, -1):
        hand(-4 * d)
    arrived("ty", yrecv, {"tm": ty})
    res = tsame[...] + yrecv[...].astype(F32)
    for i in range(2):
        out[0, i] = res[i * FP : i * FP + FR].reshape(ROWS, COLS, CH).astype(BF16)
    for h in (1, 2, 3, 4):
        for d in (1, -1):
            if d * h != -4:
                arrived(f"b{d}_{h}", slot(-d * (h + 4)), zdev(-d * h))
                hand(-d * (h + 4))
    for s in range(-8, 8):
        arrived(f"yf{s}", gath.at[at_z(s), other_z, :], yhd)
    for j in range(12):
        k, a, b = j // 4, j // 2 % 2, j % 2
        gout[k, pl.ds(b * ZR, ZR), pl.ds(128 * a, 128)] = gath[j].astype(F32)
    for b in range(2):
        v = gath[12 + b].astype(F32)
        gout[0, pl.ds(b * ZR, ZR), pl.ds(256, 64)] = v[:, :64]
        gout[1, pl.ds(b * ZR, ZR), pl.ds(256, 64)] = v[:, 64:]
    v = gath[14].astype(F32)
    gout[2, pl.ds(0, ZR), pl.ds(256, 64)] = v[:, :64]
    gout[2, pl.ds(ZR, ZR), pl.ds(256, 64)] = v[:, 64:]
    for c in started:
        c.wait_send()


def body(activations, norm_gain, norm_bias, spatial_weight, temporal_weight, cotangent):
    vm = pl.BlockSpec(memory_space=pltpu.VMEM)
    hbm = pl.BlockSpec(memory_space=pltpu.HBM)
    V = pltpu.VMEM
    zc = (HZ, 128)
    scratch = [
        V((1, 2, ROWS, COLS, CH), BF16),
        V((1, 2, ROWS, COLS, CH), BF16),
        V((9, CH, CH), BF16),
        V((3, CH, CH), BF16),
        V((CH,), F32),
        V((CH,), F32),
        V((4, 8, CH), F32),
        V((8, HR + 2 * PCOLS, CH), BF16),
        V((8 * FP, CH), BF16),
        V((2, 3, FP, CH), BF16),
        V((2, CUT, CH), BF16),
        V((2, FP - CUT, CH), BF16),
        V((2, 2, FP, CH), BF16),
        V((10 * FP, CH), BF16),
        V((16, ZR, 128), F32),
        V((8,) + zc, BF16),
        V((8,) + zc, BF16),
        V((8,) + zc, BF16),
        V((8,) + zc, BF16),
        V((16,) + zc, BF16),
        V((16,) + zc, BF16),
        V((16, ZR, 128), BF16),
        V((4, FP, CH), F32),
        V((FP, CH), F32),
        V((2 * FP, CH), F32),
        V((2 * FP, CH), F32),
        V((2 * FP, CH), F32),
        V((2 * FP, CH), F32),
        V((2 * FP, CH), BF16),
        V((2 * FP, CH), BF16),
        pltpu.SemaphoreType.DMA((6,)),
        pltpu.SemaphoreType.DMA((112,)),
        pltpu.SemaphoreType.DMA((112,)),
    ]
    return pl.pallas_call(
        kernel,
        out_shape=(
            jax.ShapeDtypeStruct((1, 2, ROWS, COLS, CH), BF16),
            jax.ShapeDtypeStruct((3, CH, CH), F32),
        ),
        in_specs=[hbm] * 6,
        out_specs=(vm, vm),
        scratch_shapes=scratch,
        compiler_params=pltpu.CompilerParams(
            collective_id=0, has_side_effects=True, vmem_limit_bytes=48 * 2**20
        ),
        name="block",
    )(
        *(
            pltpu.with_memory_space_constraint(v, pltpu.HBM)
            for v in (
                activations, norm_gain, norm_bias, spatial_weight, temporal_weight, cotangent,
            )
        )
    )


def solution(mesh):
    in_specs = (
        P("dp", "tm", None, None, "mp"),
        P("mp"),
        P("mp"),
        P(None, "mp", "tm"),
        P(None, "tm", "mp"),
        P("dp", "tm", None, None, "mp"),
    )
    out_specs = (P("dp", "tm", None, None, "mp"), P(None, "tm", "mp"))
    return jax.shard_map(body, mesh=mesh, in_specs=in_specs, out_specs=out_specs, check_vma=False)
```

```python
import jax
import jax.numpy as jnp
from jax import lax
from jax.experimental import pallas as pl
from jax.experimental.pallas import tpu as pltpu
from jax.sharding import PartitionSpec as P

MESH = pl.DeviceIdType.MESH
F32, BF16 = jnp.float32, jnp.bfloat16

CH = 320
GROUP = 40
ROWS, COLS, PCOLS = 5, 40, 48
FR = ROWS * COLS
FP = 208
DT, DL = 240, 288
DR = DT + DL
HR = ROWS * PCOLS
ZR = 160
HZ = ZR // 2
EPS = 1e-05


def dot(a, b, **kw):
    return jnp.dot(a, b, preferred_element_type=F32, **kw)


def kernel(
    act, gain, bias, ws, wt, cot, out, gout,
    actv, cotv, wsv, wtv, gainv, biasv, stats, hid, cotp, part, far_r, far_l, near, spat,
    grad, sr, sl, rr, rl, yhs, yhr, gath, hold, mine, dsp, gacc,
    tpre, tsame, tsend0, tsend1, ysend, yrecv, lsem, ssem, rsem,
):
    dp, tm, mp = lax.axis_index("dp"), lax.axis_index("tm"), lax.axis_index("mp")
    core, yl = lax.rem(tm, 2), lax.div(tm, 2)
    z, yh = lax.div(dp, 2), lax.rem(dp, 2)
    tc = tm + 1 - 2 * core
    ty = lax.rem(tm + 2, 4)
    tyc = lax.rem(tc + 2, 4)

    def zdev(s):
        return {"dp": lax.rem(dp + (2 * s + 32), 32)}

    def xdev(s):
        return {"mp": lax.rem(mp + (s + 4), 4)}

    names = {}

    def rc(name, src, dst, dev):
        i = names.setdefault(name, len(names))
        return pltpu.make_async_remote_copy(
            src_ref=src, dst_ref=dst, send_sem=ssem.at[i], recv_sem=rsem.at[i],
            device_id=dev, device_id_type=MESH,
        )

    started = []

    def send(name, src, dst, dev):
        c = rc(name, src, dst, dev)
        c.start()
        started.append(c)

    def arrived(name, dst, dev):
        rc(name, dst, dst, dev).wait_recv()

    c_act = pltpu.make_async_copy(act, actv, lsem.at[0])
    c_ws = pltpu.make_async_copy(ws, wsv, lsem.at[1])
    c_cot = pltpu.make_async_copy(cot, cotv, lsem.at[2])
    c_wt = pltpu.make_async_copy(wt, wtv, lsem.at[3])
    c_gain = pltpu.make_async_copy(gain, gainv, lsem.at[4])
    c_bias = pltpu.make_async_copy(bias, biasv, lsem.at[5])
    for c in (c_act, c_gain, c_bias, c_cot, c_ws, c_wt):
        c.start()
    yhd = {"dp": dp + 1 - 2 * yh}
    peers = [{"tm": tc}, {"tm": ty}, {"tm": tyc}, xdev(1), xdev(-1)]
    peers += [zdev(h) for h in (1, 2, 3, 4, -1, -2, -3, -4)] + [yhd]
    barrier = pltpu.get_barrier_semaphore()
    for p in peers:
        pl.semaphore_signal(barrier, inc=1, device_id=p, device_id_type=MESH)

    zrows = jnp.zeros((8, PCOLS, CH), BF16)
    hid[:, pl.ds(0, PCOLS), :] = zrows
    hid[:, pl.ds(PCOLS + HR, PCOLS), :] = zrows
    for end in (0, 9):
        spat[pl.ds(end * FP, FP), :] = jnp.zeros((FP, CH), BF16)
        cotp[pl.ds(end * FP, FP), :] = jnp.zeros((FP, CH), BF16)
    grad[15] = jnp.zeros((ZR, 128), F32)

    c_act.wait()
    x = actv[...].astype(F32).reshape(2 * FR, CH)
    ssum = jnp.sum(x, axis=0, keepdims=True)
    cen = x - ssum * (1.0 / (2 * FR))
    m2 = jnp.sum(cen * cen, axis=0, keepdims=True)
    r8 = lax.broadcasted_iota(jnp.int32, (8, CH), 0)
    stats[tm] = jnp.where(r8 == 0, ssum, jnp.where(r8 == 1, m2, 0.0))

    pl.semaphore_wait(barrier, len(peers))
    send("st_c", stats.at[tm], stats.at[tm], {"tm": tc})
    send("st_y", stats.at[tm], stats.at[tm], {"tm": ty})
    send("st_yc", stats.at[tm], stats.at[tm], {"tm": tyc})

    gi = lax.broadcasted_iota(jnp.int32, (CH, CH), 0)
    gj = lax.broadcasted_iota(jnp.int32, (CH, CH), 1)
    same = (((gi * 1639) >> 16) == ((gj * 1639) >> 16)).astype(F32)

    c_cot.wait()
    zpad = jnp.zeros((FP - FR, CH), F32)
    for i in range(2):
        cf = cotv[0, i].astype(F32).reshape(FR, CH)
        cotp[pl.ds(pl.multiple_of((2 * tm + i + 1) * FP, FP), FP), :] = jnp.concatenate(
            [cf, zpad], axis=0
        ).astype(BF16)

    arrived("st_c", stats.at[tc], {"tm": tc})
    arrived("st_y", stats.at[ty], {"tm": ty})
    arrived("st_yc", stats.at[tyc], {"tm": tyc})
    st = [stats[i] for i in range(4)]
    total = st[0] + st[1] + st[2] + st[3]
    hi = lax.Precision.HIGHEST
    avg = dot(total, same, precision=hi)[0:1] * (1.0 / (8 * FR * GROUP))
    m2all = total[1:2]
    for i in range(4):
        dm = st[i][0:1] * (1.0 / (2 * FR)) - avg
        m2all = m2all + (2.0 * FR) * dm * dm
    m2all = jnp.broadcast_to(m2all, (8, CH))
    var = dot(m2all, same, precision=hi)[0:1] * (1.0 / (8 * FR * GROUP))
    c_gain.wait()
    c_bias.wait()
    inv = lax.rsqrt(var + EPS) * gainv[...].reshape(1, CH)
    bia = biasv[...].reshape(1, CH)

    for i in range(2):
        xf = actv[0, i].astype(F32).reshape(FR, CH)
        nf = (xf - avg) * inv + bia
        hf = nf * (1.0 / (1.0 + jnp.exp(-nf)))
        hf = jnp.concatenate(
            [hf.reshape(ROWS, COLS, CH), jnp.zeros((ROWS, PCOLS - COLS, CH), F32)], axis=1
        )
        hid[2 * tm + i, pl.ds(PCOLS, HR), :] = hf.reshape(HR, CH).astype(BF16)
        own = hid.at[2 * tm + i, pl.ds(PCOLS, HR), :]
        send(f"hy{i}", own, own, {"tm": ty})
        send(f"hc{i}", own, own, {"tm": tc})

    def cframes(t):
        return cotp.at[pl.ds(pl.multiple_of((2 * t + 1) * FP, FP), 2 * FP), :]

    def hframe(f):
        return hid.at[f, pl.ds(PCOLS, HR), :]

    def relay_hidden(i):
        return rc(f"hr{i}", hframe(2 * ty + i), hframe(2 * ty + i), {"tm": tc})

    def conv(f):
        acc = []
        for b in range(3):
            v = dot(hid[f, pl.ds(0, HR), :], wsv[b])
            for a in (1, 2):
                v = v + dot(hid[f, pl.ds(PCOLS * a, HR), :], wsv[3 * a + b])
            acc.append(v)
        o = acc[1] + pltpu.roll(acc[0], 1, 0) + pltpu.roll(acc[2], HR - 1, 0)
        o = o.reshape(ROWS, PCOLS, CH)[:, :COLS, :].reshape(FR, CH)
        return jnp.concatenate([o, zpad], axis=0)

    top, low = pl.ds(0, DT), pl.ds(DT, DL)

    def pack(j, v):
        t = v[:, 256:]
        hold[j, pl.ds(0, 96)] = v[:96, :128]
        hold[j, pl.ds(96, 96)] = v[:96, 128:256]
        hold[j, pl.ds(192, 48)] = jnp.concatenate([t[:48], t[48:96]], axis=1)
        hold[j, pl.ds(240, 112)] = v[96:, :128]
        hold[j, pl.ds(352, 112)] = v[96:, 128:256]
        last = jnp.concatenate([t[160:], jnp.zeros((16, 64), F32)], axis=0)
        hold[j, pl.ds(464, 64)] = jnp.concatenate([t[96:160], last], axis=1)

    def unpack(base):
        def step(i, _):
            f = base + i
            r = (f + 1) * FP

            def put(lo, n, lane, width, v):
                spat[pl.ds(pl.multiple_of(r + lo, 16), n), pl.ds(lane, width)] = v

            put(0, 96, 0, 128, dsp[f, pl.ds(0, 96)])
            put(0, 96, 128, 128, dsp[f, pl.ds(96, 96)])
            t = dsp[f, pl.ds(192, 48)].astype(F32)
            put(0, 48, 256, 64, t[:, :64].astype(BF16))
            put(48, 48, 256, 64, t[:, 64:].astype(BF16))
            put(96, 112, 0, 128, dsp[f, pl.ds(240, 112)])
            put(96, 112, 128, 128, dsp[f, pl.ds(352, 112)])
            t = dsp[f, pl.ds(464, 64)].astype(F32)
            put(96, 64, 256, 64, t[:, :64].astype(BF16))
            put(160, 48, 256, 64, t[:48, 64:].astype(BF16))
            return 0

        lax.fori_loop(0, 4, step, 0)

    def far(h):
        return (
            rc(f"fr{h}", part.at[h, 0, top], far_r.at[h], xdev(1)),
            rc(f"fl{h}", part.at[h, 0, low], far_l.at[h], xdev(-1)),
        )

    def near_early(h):
        return (
            rc(f"nrl{h}", part.at[h, 1, low], near.at[h, 0, low], xdev(1)),
            rc(f"nlt{h}", part.at[h, 2, top], near.at[h, 1, top], xdev(-1)),
        )

    def gathers(h, base):
        f = base + mp
        t, b = dsp.at[f, top], dsp.at[f, low]
        return (
            rc(f"grt{h}", t, t, xdev(1)),
            rc(f"glb{h}", b, b, xdev(-1)),
            rc(f"grb{h}", b, b, xdev(1)),
            rc(f"glt{h}", t, t, xdev(-1)),
        )

    def half_convs(h, base, hook):
        def step(j, _):
            q, r = lax.div(j, 2), lax.rem(j, 2)
            off = 2 + q - r - 2 * q * r
            pack(j, conv(base + lax.rem(mp + off, 4)))

            @pl.when(j == 0)
            def _():
                part[h, 0] = hold[0].astype(BF16)
                for c in far(h):
                    c.start()

            @pl.when(j == 1)
            def _():
                part[h, 1, low] = hold[1, low].astype(BF16)
                near_early(h)[0].start()

            @pl.when(j == 2)
            def _():
                part[h, 2, top] = hold[2, top].astype(BF16)
                near_early(h)[1].start()

            hook(j)
            return 0

        lax.fori_loop(0, 4, step, 0)
        started.extend(far(h))
        started.extend(near_early(h))

    def half_near(h):
        arrived(f"fr{h}", far_r.at[h], xdev(-1))
        part[h, 1, top] = (hold[1, top] + far_r[h].astype(F32)).astype(BF16)
        send(f"nrt{h}", part.at[h, 1, top], near.at[h, 0, top], xdev(1))
        arrived(f"fl{h}", far_l.at[h], xdev(1))
        part[h, 2, low] = (hold[2, low] + far_l[h].astype(F32)).astype(BF16)
        send(f"nll{h}", part.at[h, 2, low], near.at[h, 1, low], xdev(-1))
        mine[...] = hold[3]

    def half_sum(h, base):
        arrived(f"nrl{h}", near.at[h, 0, low], xdev(-1))
        arrived(f"nlt{h}", near.at[h, 1, top], xdev(1))
        arrived(f"nrt{h}", near.at[h, 0, top], xdev(-1))
        arrived(f"nll{h}", near.at[h, 1, low], xdev(1))
        whole = mine[...] + near[h, 0].astype(F32) + near[h, 1].astype(F32)
        dsp[base + mp] = whole.astype(BF16)
        for c in gathers(h, base):
            c.start()

    def forwards(h, base):
        lf, rf = base + lax.rem(mp + 3, 4), base + lax.rem(mp + 1, 4)
        return (
            rc(f"wr{h}", dsp.at[lf, top], dsp.at[lf, top], xdev(1)),
            rc(f"wl{h}", dsp.at[rf, low], dsp.at[rf, low], xdev(-1)),
        )

    def half_forward(h, base):
        lf, rf = base + lax.rem(mp + 3, 4), base + lax.rem(mp + 1, 4)
        to_r, to_l = forwards(h, base)
        arrived(f"grt{h}", dsp.at[lf, top], xdev(-1))
        to_r.start()
        arrived(f"glb{h}", dsp.at[rf, low], xdev(1))
        to_l.start()

    def half_done(h, base):
        lf, rf = base + lax.rem(mp + 3, 4), base + lax.rem(mp + 1, 4)
        ff = base + lax.rem(mp + 2, 4)
        arrived(f"grb{h}", dsp.at[lf, low], xdev(-1))
        arrived(f"glt{h}", dsp.at[rf, top], xdev(1))
        arrived(f"wr{h}", dsp.at[ff, top], xdev(-1))
        arrived(f"wl{h}", dsp.at[ff, low], xdev(1))

    base0, base1 = 4 * yl, 4 * (1 - yl)
    c_ws.wait()
    for i in range(2):
        arrived(f"hc{i}", hframe(2 * tc + i), {"tm": tc})

    half_convs(0, base0, lambda j: None)
    half_near(0)
    for i in range(2):
        arrived(f"hy{i}", hframe(2 * ty + i), {"tm": ty})
        c = relay_hidden(i)
        c.start()
        started.append(c)
    send("cy", cframes(tm), cframes(tm), {"tm": ty})
    for i in range(2):
        arrived(f"hr{i}", hframe(2 * tyc + i), {"tm": tc})

    def between(j):
        @pl.when(j == 1)
        def _():
            half_sum(0, base0)

    half_convs(1, base1, between)
    started.extend(gathers(0, base0))
    half_near(1)
    send("cc", cframes(tm), cframes(tm), {"tm": tc})
    half_forward(0, base0)
    started.extend(forwards(0, base0))
    half_sum(1, base1)
    started.extend(gathers(1, base1))
    arrived("cc", cframes(tc), {"tm": tc})
    arrived("cy", cframes(ty), {"tm": ty})
    send("cr", cframes(ty), cframes(ty), {"tm": tc})
    half_done(0, base0)
    unpack(base0)
    half_forward(1, base1)
    started.extend(forwards(1, base1))
    arrived("cr", cframes(tyc), {"tm": tc})
    def half_grad(k, base):
        return lax.dot_general(
            spat[pl.ds(pl.multiple_of((base + 1) * FP, FP), 4 * FP), :],
            cotp[pl.ds(pl.multiple_of((base + 2 - k) * FP, FP), 4 * FP), :],
            (((0,), (0,)), ((), ())),
            preferred_element_type=F32,
        )

    for k in range(3):
        gacc[k] = half_grad(k, base0)
    half_done(1, base1)
    unpack(base1)
    c_wt.wait()

    tails = []
    for k in range(3):
        g = gacc[k] + half_grad(k, base1)
        for a in range(2):
            grad[pl.ds(4 * k + 2 * a, 2)] = g[:, 128 * a : 128 * a + 128].reshape(2, ZR, 128)
        tails.append(g[:, 256:])
    grad[pl.ds(12, 2)] = jnp.concatenate(tails[:2], axis=1).reshape(2, ZR, 128)
    grad[14] = jnp.concatenate([tails[2][:ZR], tails[2][ZR:]], axis=1)

    order = (8, 7, -7, 6, -6, 5, -5, 4, -4, 3, -3, 2, -2, 1, -1, 0)
    bounds = (0, 3, 7, 11, 15, 16)
    mine_z = pl.ds(pl.multiple_of(yh * HZ, HZ), HZ)
    other_z = pl.ds(pl.multiple_of((1 - yh) * HZ, HZ), HZ)

    def at_z(s):
        return lax.rem(z + (s + 32), 16)

    def group(g):
        return pl.ds(bounds[g], bounds[g + 1] - bounds[g])

    def send_group(g):
        for p in range(bounds[g], bounds[g + 1]):
            yhs[p] = grad[at_z(order[p]), other_z, :].astype(BF16)
        send(f"yg{g}", yhs.at[group(g)], yhr.at[group(g)], yhd)

    send_group(0)
    send_group(1)
    got = set()

    def own(s):
        p = order.index(s)
        g = max(i for i in range(5) if bounds[i] <= p)
        if g not in got:
            got.add(g)
            arrived(f"yg{g}", yhr.at[group(g)], yhd)
            if g < 3:
                send_group(g + 2)
        return grad[at_z(s), mine_z, :] + yhr[p].astype(F32)

    ways = ((1, sr, rr), (-1, sl, rl))

    def hops(i):
        return i - 4 if i > 4 else i

    def terms(*far_to_near):
        for i in far_to_near:
            for d, snd, rcv in ways[: 1 if i == 8 else 2]:
                snd[i - 1] = own(d * i).astype(BF16)
                send(f"z{d}_{i}", snd.at[i - 1], rcv.at[i - 1], zdev(d * hops(i)))

    def incoming(d, rcv, steps):
        v = None
        for i in steps:
            if d * i != -8:
                arrived(f"z{d}_{i}", rcv.at[i - 1], zdev(-d * hops(i)))
                t = rcv[i - 1].astype(F32)
                v = t if v is None else v + t
        return v

    def temporal(t):
        r0 = pl.multiple_of(2 * t * FP, FP)
        v = dot(spat[pl.ds(r0, 2 * FP), :], wtv[0])
        for k in (1, 2):
            v = v + dot(spat[pl.ds(pl.multiple_of(r0 + k * FP, FP), 2 * FP), :], wtv[k])
        return v

    tsend0[...] = temporal(tyc)
    send("tp", tsend0, tpre, {"tm": tc})
    terms(8, 7, 6, 5)
    tsend1[...] = temporal(tc)
    send("ts", tsend1, tsame, {"tm": tc})
    terms(3, 2, 1)
    for d, snd, rcv in ways:
        snd[3] = (own(4 * d) + incoming(d, rcv, (5, 6, 7, 8))).astype(BF16)
        send(f"z{d}_4", snd.at[3], rcv.at[3], zdev(4 * d))
    tacc = temporal(ty)
    arrived("tp", tpre, {"tm": tc})
    ysend[...] = (tacc + tpre[...]).astype(BF16)
    send("ty", ysend, yrecv, {"tm": ty})
    tsend_own = temporal(tm)
    arrived("ts", tsame, {"tm": tc})
    tsame[...] = tsame[...] + tsend_own
    zsum = own(0)
    for d, snd, rcv in ways:
        zsum = zsum + incoming(d, rcv, (1, 2, 3, 4))
    gath[z, mine_z, :] = (zsum * (1.0 / 32.0)).astype(BF16)

    def slot(s):
        return gath.at[at_z(s), mine_z, :]

    def hand(s):
        send(f"yf{s}", slot(s), slot(s), yhd)

    for h in (4, 3, 2, 1):
        for d in (1, -1):
            send(f"a{d}_{h}", slot(0), slot(0), zdev(d * h))
    hand(0)
    for h in (1, 2, 3):
        for d in (1, -1):
            arrived(f"a{d}_{h}", slot(-d * h), zdev(-d * h))
            hand(-d * h)
    for d in (1, -1):
        arrived(f"a{d}_4", slot(-4 * d), zdev(-4 * d))
        for h in (4, 3, 2, 1):
            if d * h != -4:
                send(f"b{d}_{h}", slot(-4 * d), slot(-4 * d), zdev(d * h))
    for d in (1, -1):
        hand(-4 * d)
    arrived("ty", yrecv, {"tm": ty})
    res = tsame[...] + yrecv[...].astype(F32)
    for i in range(2):
        out[0, i] = res[i * FP : i * FP + FR].reshape(ROWS, COLS, CH).astype(BF16)
    for h in (1, 2, 3, 4):
        for d in (1, -1):
            if d * h != -4:
                arrived(f"b{d}_{h}", slot(-d * (h + 4)), zdev(-d * h))
                hand(-d * (h + 4))
    for s in range(-8, 8):
        arrived(f"yf{s}", gath.at[at_z(s), other_z, :], yhd)
    for j in range(12):
        k, a, b = j // 4, j // 2 % 2, j % 2
        gout[k, pl.ds(b * ZR, ZR), pl.ds(128 * a, 128)] = gath[j].astype(F32)
    for b in range(2):
        v = gath[12 + b].astype(F32)
        gout[0, pl.ds(b * ZR, ZR), pl.ds(256, 64)] = v[:, :64]
        gout[1, pl.ds(b * ZR, ZR), pl.ds(256, 64)] = v[:, 64:]
    v = gath[14].astype(F32)
    gout[2, pl.ds(0, ZR), pl.ds(256, 64)] = v[:, :64]
    gout[2, pl.ds(ZR, ZR), pl.ds(256, 64)] = v[:, 64:]
    for c in started:
        c.wait_send()


def body(activations, norm_gain, norm_bias, spatial_weight, temporal_weight, cotangent):
    vm = pl.BlockSpec(memory_space=pltpu.VMEM)
    hbm = pl.BlockSpec(memory_space=pltpu.HBM)
    V = pltpu.VMEM
    zc = (HZ, 128)
    scratch = [
        V((1, 2, ROWS, COLS, CH), BF16),
        V((1, 2, ROWS, COLS, CH), BF16),
        V((9, CH, CH), BF16),
        V((3, CH, CH), BF16),
        V((CH,), F32),
        V((CH,), F32),
        V((4, 8, CH), F32),
        V((8, HR + 2 * PCOLS, CH), BF16),
        V((10 * FP, CH), BF16),
        V((2, 3, DR, 128), BF16),
        V((2, DT, 128), BF16),
        V((2, DL, 128), BF16),
        V((2, 2, DR, 128), BF16),
        V((10 * FP, CH), BF16),
        V((16, ZR, 128), F32),
        V((8,) + zc, BF16),
        V((8,) + zc, BF16),
        V((8,) + zc, BF16),
        V((8,) + zc, BF16),
        V((16,) + zc, BF16),
        V((16,) + zc, BF16),
        V((16, ZR, 128), BF16),
        V((4, DR, 128), F32),
        V((DR, 128), F32),
        V((8, DR, 128), BF16),
        V((3, CH, CH), F32),
        V((2 * FP, CH), F32),
        V((2 * FP, CH), F32),
        V((2 * FP, CH), F32),
        V((2 * FP, CH), F32),
        V((2 * FP, CH), BF16),
        V((2 * FP, CH), BF16),
        pltpu.SemaphoreType.DMA((6,)),
        pltpu.SemaphoreType.DMA((112,)),
        pltpu.SemaphoreType.DMA((112,)),
    ]
    return pl.pallas_call(
        kernel,
        out_shape=(
            jax.ShapeDtypeStruct((1, 2, ROWS, COLS, CH), BF16),
            jax.ShapeDtypeStruct((3, CH, CH), F32),
        ),
        in_specs=[hbm] * 6,
        out_specs=(vm, vm),
        scratch_shapes=scratch,
        compiler_params=pltpu.CompilerParams(
            collective_id=0, has_side_effects=True, vmem_limit_bytes=48 * 2**20
        ),
        name="block",
    )(
        *(
            pltpu.with_memory_space_constraint(v, pltpu.HBM)
            for v in (
                activations, norm_gain, norm_bias, spatial_weight, temporal_weight, cotangent,
            )
        )
    )


def solution(mesh):
    in_specs = (
        P("dp", "tm", None, None, "mp"),
        P("mp"),
        P("mp"),
        P(None, "mp", "tm"),
        P(None, "tm", "mp"),
        P("dp", "tm", None, None, "mp"),
    )
    out_specs = (P("dp", "tm", None, None, "mp"), P(None, "tm", "mp"))
    return jax.shard_map(body, mesh=mesh, in_specs=in_specs, out_specs=out_specs, check_vma=False)
```

```python
import jax
import jax.numpy as jnp
from jax import lax
from jax.experimental import pallas as pl
from jax.experimental.pallas import tpu as pltpu
from jax.sharding import PartitionSpec as P

MESH = pl.DeviceIdType.MESH
F32, BF16 = jnp.float32, jnp.bfloat16

CH = 320
GROUP = 40
ROWS, COLS, PCOLS = 5, 40, 48
FR = ROWS * COLS
FP = 208
DT, DL = 240, 288
DR = DT + DL
HR = ROWS * PCOLS
ZR = 160
HZ = ZR // 2
EPS = 1e-05


def dot(a, b, **kw):
    return jnp.dot(a, b, preferred_element_type=F32, **kw)


def kernel(
    act, gain, bias, ws, wt, cot, out, gout,
    actv, cotv, wsv, wtv, gainv, biasv, stats, hid, cotp, part, far_r, far_l, near, spat,
    grad, sr, sl, rr, rl, yhs, yhr, gath, hold, mine, dsp, gacc,
    tpre, tsame, tsend0, tsend1, ysend, yrecv, lsem, ssem, rsem,
):
    dp, tm, mp = lax.axis_index("dp"), lax.axis_index("tm"), lax.axis_index("mp")
    core, yl = lax.rem(tm, 2), lax.div(tm, 2)
    z, yh = lax.div(dp, 2), lax.rem(dp, 2)
    tc = tm + 1 - 2 * core
    ty = lax.rem(tm + 2, 4)
    tyc = lax.rem(tc + 2, 4)

    def zdev(s):
        return {"dp": lax.rem(dp + (2 * s + 32), 32)}

    def xdev(s):
        return {"mp": lax.rem(mp + (s + 4), 4)}

    names = {}

    def rc(name, src, dst, dev):
        i = names.setdefault(name, len(names))
        return pltpu.make_async_remote_copy(
            src_ref=src, dst_ref=dst, send_sem=ssem.at[i], recv_sem=rsem.at[i],
            device_id=dev, device_id_type=MESH,
        )

    started = []

    def send(name, src, dst, dev):
        c = rc(name, src, dst, dev)
        c.start()
        started.append(c)

    def arrived(name, dst, dev):
        rc(name, dst, dst, dev).wait_recv()

    c_act = pltpu.make_async_copy(act, actv, lsem.at[0])
    c_ws = pltpu.make_async_copy(ws, wsv, lsem.at[1])
    c_cot = pltpu.make_async_copy(cot, cotv, lsem.at[2])
    c_wt = pltpu.make_async_copy(wt, wtv, lsem.at[3])
    c_gain = pltpu.make_async_copy(gain, gainv, lsem.at[4])
    c_bias = pltpu.make_async_copy(bias, biasv, lsem.at[5])
    for c in (c_act, c_gain, c_bias):
        c.start()
    yhd = {"dp": dp + 1 - 2 * yh}
    peers = [{"tm": tc}, {"tm": ty}, {"tm": tyc}, xdev(1), xdev(-1)]
    peers += [zdev(h) for h in (1, 2, 3, 4, -1, -2, -3, -4)] + [yhd]
    barrier = pltpu.get_barrier_semaphore()
    for p in peers:
        pl.semaphore_signal(barrier, inc=1, device_id=p, device_id_type=MESH)

    zrows = jnp.zeros((8, PCOLS, CH), BF16)
    hid[:, pl.ds(0, PCOLS), :] = zrows
    hid[:, pl.ds(PCOLS + HR, PCOLS), :] = zrows
    for end in (0, 9):
        spat[pl.ds(end * FP, FP), :] = jnp.zeros((FP, CH), BF16)
        cotp[pl.ds(end * FP, FP), :] = jnp.zeros((FP, CH), BF16)
    grad[15] = jnp.zeros((ZR, 128), F32)

    c_act.wait()
    for c in (c_cot, c_ws, c_wt):
        c.start()
    x = actv[...].astype(F32).reshape(2 * FR, CH)
    ssum = jnp.sum(x, axis=0, keepdims=True)
    cen = x - ssum * (1.0 / (2 * FR))
    m2 = jnp.sum(cen * cen, axis=0, keepdims=True)
    r8 = lax.broadcasted_iota(jnp.int32, (8, CH), 0)
    stats[tm] = jnp.where(r8 == 0, ssum, jnp.where(r8 == 1, m2, 0.0))

    pl.semaphore_wait(barrier, len(peers))
    send("st_c", stats.at[tm], stats.at[tm], {"tm": tc})
    send("st_y", stats.at[tm], stats.at[tm], {"tm": ty})
    send("st_yc", stats.at[tm], stats.at[tm], {"tm": tyc})

    gi = lax.broadcasted_iota(jnp.int32, (CH, CH), 0)
    gj = lax.broadcasted_iota(jnp.int32, (CH, CH), 1)
    same = (((gi * 1639) >> 16) == ((gj * 1639) >> 16)).astype(F32).astype(BF16)

    def group_sums(v):
        p1 = v.astype(BF16).astype(F32)
        p2 = (v - p1).astype(BF16).astype(F32)
        p3 = v - p1 - p2
        parts = jnp.concatenate([p1, p2, p3, jnp.zeros_like(v)], axis=0)
        o = dot(parts.astype(BF16), same)
        return (o[0:8] + o[8:16] + o[16:24])[0:1]

    c_cot.wait()
    zpad = jnp.zeros((FP - FR, CH), F32)
    for i in range(2):
        cf = cotv[0, i].astype(F32).reshape(FR, CH)
        cotp[pl.ds(pl.multiple_of((2 * tm + i + 1) * FP, FP), FP), :] = jnp.concatenate(
            [cf, zpad], axis=0
        ).astype(BF16)

    arrived("st_c", stats.at[tc], {"tm": tc})
    arrived("st_y", stats.at[ty], {"tm": ty})
    arrived("st_yc", stats.at[tyc], {"tm": tyc})
    st = [stats[i] for i in range(4)]
    total = st[0] + st[1] + st[2] + st[3]
    avg = group_sums(total) * (1.0 / (8 * FR * GROUP))
    m2all = total[1:2]
    for i in range(4):
        dm = st[i][0:1] * (1.0 / (2 * FR)) - avg
        m2all = m2all + (2.0 * FR) * dm * dm
    m2all = jnp.broadcast_to(m2all, (8, CH))
    var = group_sums(m2all) * (1.0 / (8 * FR * GROUP))
    c_gain.wait()
    c_bias.wait()
    inv = lax.rsqrt(var + EPS) * gainv[...].reshape(1, CH)
    bia = biasv[...].reshape(1, CH)

    for i in range(2):
        xf = actv[0, i].astype(F32).reshape(FR, CH)
        nf = (xf - avg) * inv + bia
        hf = nf * (1.0 / (1.0 + jnp.exp(-nf)))
        hf = jnp.concatenate(
            [hf.reshape(ROWS, COLS, CH), jnp.zeros((ROWS, PCOLS - COLS, CH), F32)], axis=1
        )
        hid[2 * tm + i, pl.ds(PCOLS, HR), :] = hf.reshape(HR, CH).astype(BF16)
        own = hid.at[2 * tm + i, pl.ds(PCOLS, HR), :]
        send(f"hy{i}", own, own, {"tm": ty})
        send(f"hc{i}", own, own, {"tm": tc})

    def cframes(t):
        return cotp.at[pl.ds(pl.multiple_of((2 * t + 1) * FP, FP), 2 * FP), :]

    def hframe(f):
        return hid.at[f, pl.ds(PCOLS, HR), :]

    def relay_hidden(i):
        return rc(f"hr{i}", hframe(2 * ty + i), hframe(2 * ty + i), {"tm": tc})

    def conv(f):
        acc = []
        for b in range(3):
            v = dot(hid[f, pl.ds(0, HR), :], wsv[b])
            for a in (1, 2):
                v = v + dot(hid[f, pl.ds(PCOLS * a, HR), :], wsv[3 * a + b])
            acc.append(v)
        o = acc[1] + pltpu.roll(acc[0], 1, 0) + pltpu.roll(acc[2], HR - 1, 0)
        o = o.reshape(ROWS, PCOLS, CH)[:, :COLS, :].reshape(FR, CH)
        return jnp.concatenate([o, zpad], axis=0)

    top, low = pl.ds(0, DT), pl.ds(DT, DL)

    def pack(j, v):
        t = v[:, 256:]
        hold[j, pl.ds(0, 96)] = v[:96, :128]
        hold[j, pl.ds(96, 96)] = v[:96, 128:256]
        hold[j, pl.ds(192, 48)] = jnp.concatenate([t[:48], t[48:96]], axis=1)
        hold[j, pl.ds(240, 112)] = v[96:, :128]
        hold[j, pl.ds(352, 112)] = v[96:, 128:256]
        last = jnp.concatenate([t[160:], jnp.zeros((16, 64), F32)], axis=0)
        hold[j, pl.ds(464, 64)] = jnp.concatenate([t[96:160], last], axis=1)

    def unpack(base):
        def step(i, _):
            f = base + i
            r = (f + 1) * FP

            def put(lo, n, lane, width, v):
                spat[pl.ds(pl.multiple_of(r + lo, 16), n), pl.ds(lane, width)] = v

            put(0, 96, 0, 128, dsp[f, pl.ds(0, 96)])
            put(0, 96, 128, 128, dsp[f, pl.ds(96, 96)])
            t = dsp[f, pl.ds(192, 48)].astype(F32)
            put(0, 48, 256, 64, t[:, :64].astype(BF16))
            put(48, 48, 256, 64, t[:, 64:].astype(BF16))
            put(96, 112, 0, 128, dsp[f, pl.ds(240, 112)])
            put(96, 112, 128, 128, dsp[f, pl.ds(352, 112)])
            t = dsp[f, pl.ds(464, 64)].astype(F32)
            put(96, 64, 256, 64, t[:, :64].astype(BF16))
            put(160, 48, 256, 64, t[:48, 64:].astype(BF16))
            return 0

        lax.fori_loop(0, 4, step, 0)

    def far(h):
        return (
            rc(f"fr{h}", part.at[h, 0, top], far_r.at[h], xdev(1)),
            rc(f"fl{h}", part.at[h, 0, low], far_l.at[h], xdev(-1)),
        )

    def near_early(h):
        return (
            rc(f"nrl{h}", part.at[h, 1, low], near.at[h, 0, low], xdev(1)),
            rc(f"nlt{h}", part.at[h, 2, top], near.at[h, 1, top], xdev(-1)),
        )

    def gathers(h, base):
        f = base + mp
        t, b = dsp.at[f, top], dsp.at[f, low]
        return (
            rc(f"grt{h}", t, t, xdev(1)),
            rc(f"glb{h}", b, b, xdev(-1)),
            rc(f"grb{h}", b, b, xdev(1)),
            rc(f"glt{h}", t, t, xdev(-1)),
        )

    def half_convs(h, base, hook):
        def step(j, _):
            q, r = lax.div(j, 2), lax.rem(j, 2)
            off = 2 + q - r - 2 * q * r
            pack(j, conv(base + lax.rem(mp + off, 4)))

            @pl.when(j == 0)
            def _():
                part[h, 0] = hold[0].astype(BF16)
                for c in far(h):
                    c.start()

            @pl.when(j == 1)
            def _():
                part[h, 1, low] = hold[1, low].astype(BF16)
                near_early(h)[0].start()

            @pl.when(j == 2)
            def _():
                part[h, 2, top] = hold[2, top].astype(BF16)
                near_early(h)[1].start()

            hook(j)
            return 0

        lax.fori_loop(0, 4, step, 0)
        started.extend(far(h))
        started.extend(near_early(h))

    def half_near(h):
        arrived(f"fr{h}", far_r.at[h], xdev(-1))
        part[h, 1, top] = (hold[1, top] + far_r[h].astype(F32)).astype(BF16)
        send(f"nrt{h}", part.at[h, 1, top], near.at[h, 0, top], xdev(1))
        arrived(f"fl{h}", far_l.at[h], xdev(1))
        part[h, 2, low] = (hold[2, low] + far_l[h].astype(F32)).astype(BF16)
        send(f"nll{h}", part.at[h, 2, low], near.at[h, 1, low], xdev(-1))
        mine[...] = hold[3]

    def half_sum(h, base):
        arrived(f"nrl{h}", near.at[h, 0, low], xdev(-1))
        arrived(f"nlt{h}", near.at[h, 1, top], xdev(1))
        arrived(f"nrt{h}", near.at[h, 0, top], xdev(-1))
        arrived(f"nll{h}", near.at[h, 1, low], xdev(1))
        whole = mine[...] + near[h, 0].astype(F32) + near[h, 1].astype(F32)
        dsp[base + mp] = whole.astype(BF16)
        for c in gathers(h, base):
            c.start()

    def forwards(h, base):
        lf, rf = base + lax.rem(mp + 3, 4), base + lax.rem(mp + 1, 4)
        return (
            rc(f"wr{h}", dsp.at[lf, top], dsp.at[lf, top], xdev(1)),
            rc(f"wl{h}", dsp.at[rf, low], dsp.at[rf, low], xdev(-1)),
        )

    def half_forward(h, base):
        lf, rf = base + lax.rem(mp + 3, 4), base + lax.rem(mp + 1, 4)
        to_r, to_l = forwards(h, base)
        arrived(f"grt{h}", dsp.at[lf, top], xdev(-1))
        to_r.start()
        arrived(f"glb{h}", dsp.at[rf, low], xdev(1))
        to_l.start()

    def half_done(h, base):
        lf, rf = base + lax.rem(mp + 3, 4), base + lax.rem(mp + 1, 4)
        ff = base + lax.rem(mp + 2, 4)
        arrived(f"grb{h}", dsp.at[lf, low], xdev(-1))
        arrived(f"glt{h}", dsp.at[rf, top], xdev(1))
        arrived(f"wr{h}", dsp.at[ff, top], xdev(-1))
        arrived(f"wl{h}", dsp.at[ff, low], xdev(1))

    base0, base1 = 4 * yl, 4 * (1 - yl)
    c_ws.wait()
    for i in range(2):
        arrived(f"hc{i}", hframe(2 * tc + i), {"tm": tc})

    half_convs(0, base0, lambda j: None)
    half_near(0)
    for i in range(2):
        arrived(f"hy{i}", hframe(2 * ty + i), {"tm": ty})
        c = relay_hidden(i)
        c.start()
        started.append(c)
    send("cy", cframes(tm), cframes(tm), {"tm": ty})
    for i in range(2):
        arrived(f"hr{i}", hframe(2 * tyc + i), {"tm": tc})

    def between(j):
        @pl.when(j == 1)
        def _():
            half_sum(0, base0)

    half_convs(1, base1, between)
    started.extend(gathers(0, base0))
    half_near(1)
    send("cc", cframes(tm), cframes(tm), {"tm": tc})
    half_forward(0, base0)
    started.extend(forwards(0, base0))
    half_sum(1, base1)
    started.extend(gathers(1, base1))
    arrived("cc", cframes(tc), {"tm": tc})
    arrived("cy", cframes(ty), {"tm": ty})
    send("cr", cframes(ty), cframes(ty), {"tm": tc})
    half_done(0, base0)
    unpack(base0)
    half_forward(1, base1)
    started.extend(forwards(1, base1))
    arrived("cr", cframes(tyc), {"tm": tc})
    def half_grad(k, base):
        return lax.dot_general(
            spat[pl.ds(pl.multiple_of((base + 1) * FP, FP), 4 * FP), :],
            cotp[pl.ds(pl.multiple_of((base + 2 - k) * FP, FP), 4 * FP), :],
            (((0,), (0,)), ((), ())),
            preferred_element_type=F32,
        )

    for k in range(3):
        gacc[k] = half_grad(k, base0)
    half_done(1, base1)
    unpack(base1)
    c_wt.wait()

    tails = []
    for k in range(3):
        g = gacc[k] + half_grad(k, base1)
        for a in range(2):
            grad[pl.ds(4 * k + 2 * a, 2)] = g[:, 128 * a : 128 * a + 128].reshape(2, ZR, 128)
        tails.append(g[:, 256:])
    grad[pl.ds(12, 2)] = jnp.concatenate(tails[:2], axis=1).reshape(2, ZR, 128)
    grad[14] = jnp.concatenate([tails[2][:ZR], tails[2][ZR:]], axis=1)

    order = (8, 7, -7, 6, -6, 5, -5, 4, -4, 3, -3, 2, -2, 1, -1, 0)
    bounds = (0, 3, 7, 11, 15, 16)
    mine_z = pl.ds(pl.multiple_of(yh * HZ, HZ), HZ)
    other_z = pl.ds(pl.multiple_of((1 - yh) * HZ, HZ), HZ)

    def at_z(s):
        return lax.rem(z + (s + 32), 16)

    def group(g):
        return pl.ds(bounds[g], bounds[g + 1] - bounds[g])

    def send_group(g):
        for p in range(bounds[g], bounds[g + 1]):
            yhs[p] = grad[at_z(order[p]), other_z, :].astype(BF16)
        send(f"yg{g}", yhs.at[group(g)], yhr.at[group(g)], yhd)

    send_group(0)
    send_group(1)
    got = set()

    def own(s):
        p = order.index(s)
        g = max(i for i in range(5) if bounds[i] <= p)
        if g not in got:
            got.add(g)
            arrived(f"yg{g}", yhr.at[group(g)], yhd)
            if g < 3:
                send_group(g + 2)
        return grad[at_z(s), mine_z, :] + yhr[p].astype(F32)

    ways = ((1, sr, rr), (-1, sl, rl))

    def hops(i):
        return i - 4 if i > 4 else i

    def terms(*far_to_near):
        for i in far_to_near:
            for d, snd, rcv in ways[: 1 if i == 8 else 2]:
                snd[i - 1] = own(d * i).astype(BF16)
                send(f"z{d}_{i}", snd.at[i - 1], rcv.at[i - 1], zdev(d * hops(i)))

    def incoming(d, rcv, steps):
        v = None
        for i in steps:
            if d * i != -8:
                arrived(f"z{d}_{i}", rcv.at[i - 1], zdev(-d * hops(i)))
                t = rcv[i - 1].astype(F32)
                v = t if v is None else v + t
        return v

    def temporal(t):
        r0 = pl.multiple_of(2 * t * FP, FP)
        v = dot(spat[pl.ds(r0, 2 * FP), :], wtv[0])
        for k in (1, 2):
            v = v + dot(spat[pl.ds(pl.multiple_of(r0 + k * FP, FP), 2 * FP), :], wtv[k])
        return v

    tsend0[...] = temporal(tyc)
    send("tp", tsend0, tpre, {"tm": tc})
    terms(8, 7, 6, 5)
    tsend1[...] = temporal(tc)
    send("ts", tsend1, tsame, {"tm": tc})
    terms(3, 2, 1)
    for d, snd, rcv in ways:
        snd[3] = (own(4 * d) + incoming(d, rcv, (5, 6, 7, 8))).astype(BF16)
        send(f"z{d}_4", snd.at[3], rcv.at[3], zdev(4 * d))
    tacc = temporal(ty)
    arrived("tp", tpre, {"tm": tc})
    ysend[...] = (tacc + tpre[...]).astype(BF16)
    send("ty", ysend, yrecv, {"tm": ty})
    tsend_own = temporal(tm)
    arrived("ts", tsame, {"tm": tc})
    tsame[...] = tsame[...] + tsend_own
    zsum = own(0)
    for d, snd, rcv in ways:
        zsum = zsum + incoming(d, rcv, (1, 2, 3, 4))
    gath[z, mine_z, :] = (zsum * (1.0 / 32.0)).astype(BF16)

    def slot(s):
        return gath.at[at_z(s), mine_z, :]

    def hand(s):
        send(f"yf{s}", slot(s), slot(s), yhd)

    for h in (4, 3, 2, 1):
        for d in (1, -1):
            send(f"a{d}_{h}", slot(0), slot(0), zdev(d * h))
    hand(0)
    for h in (1, 2, 3):
        for d in (1, -1):
            arrived(f"a{d}_{h}", slot(-d * h), zdev(-d * h))
            hand(-d * h)
    for d in (1, -1):
        arrived(f"a{d}_4", slot(-4 * d), zdev(-4 * d))
        for h in (4, 3, 2, 1):
            if d * h != -4:
                send(f"b{d}_{h}", slot(-4 * d), slot(-4 * d), zdev(d * h))
    for d in (1, -1):
        hand(-4 * d)
    arrived("ty", yrecv, {"tm": ty})
    res = tsame[...] + yrecv[...].astype(F32)
    for i in range(2):
        out[0, i] = res[i * FP : i * FP + FR].reshape(ROWS, COLS, CH).astype(BF16)
    for h in (1, 2, 3, 4):
        for d in (1, -1):
            if d * h != -4:
                arrived(f"b{d}_{h}", slot(-d * (h + 4)), zdev(-d * h))
                hand(-d * (h + 4))
    for c in started:
        c.wait_send()

    def write(sel, off):
        for j in range(12):
            k, a, b = j // 4, j // 2 % 2, j % 2
            rows = pl.ds(pl.multiple_of(off + b * ZR, 16), HZ)
            gout[k, rows, pl.ds(128 * a, 128)] = gath[j, sel, :].astype(F32)
        for b in range(2):
            rows = pl.ds(pl.multiple_of(off + b * ZR, 16), HZ)
            v = gath[12 + b, sel, :].astype(F32)
            gout[0, rows, pl.ds(256, 64)] = v[:, :64]
            gout[1, rows, pl.ds(256, 64)] = v[:, 64:]
            v = gath[14, sel, :].astype(F32)
            gout[2, rows, pl.ds(256, 64)] = v[:, 64 * b : 64 * b + 64]

    write(mine_z, yh * HZ)
    for s in range(-8, 8):
        arrived(f"yf{s}", gath.at[at_z(s), other_z, :], yhd)
    write(other_z, (1 - yh) * HZ)


def body(activations, norm_gain, norm_bias, spatial_weight, temporal_weight, cotangent):
    vm = pl.BlockSpec(memory_space=pltpu.VMEM)
    hbm = pl.BlockSpec(memory_space=pltpu.HBM)
    V = pltpu.VMEM
    zc = (HZ, 128)
    scratch = [
        V((1, 2, ROWS, COLS, CH), BF16),
        V((1, 2, ROWS, COLS, CH), BF16),
        V((9, CH, CH), BF16),
        V((3, CH, CH), BF16),
        V((CH,), F32),
        V((CH,), F32),
        V((4, 8, CH), F32),
        V((8, HR + 2 * PCOLS, CH), BF16),
        V((10 * FP, CH), BF16),
        V((2, 3, DR, 128), BF16),
        V((2, DT, 128), BF16),
        V((2, DL, 128), BF16),
        V((2, 2, DR, 128), BF16),
        V((10 * FP, CH), BF16),
        V((16, ZR, 128), F32),
        V((8,) + zc, BF16),
        V((8,) + zc, BF16),
        V((8,) + zc, BF16),
        V((8,) + zc, BF16),
        V((16,) + zc, BF16),
        V((16,) + zc, BF16),
        V((16, ZR, 128), BF16),
        V((4, DR, 128), F32),
        V((DR, 128), F32),
        V((8, DR, 128), BF16),
        V((3, CH, CH), F32),
        V((2 * FP, CH), F32),
        V((2 * FP, CH), F32),
        V((2 * FP, CH), F32),
        V((2 * FP, CH), F32),
        V((2 * FP, CH), BF16),
        V((2 * FP, CH), BF16),
        pltpu.SemaphoreType.DMA((6,)),
        pltpu.SemaphoreType.DMA((112,)),
        pltpu.SemaphoreType.DMA((112,)),
    ]
    return pl.pallas_call(
        kernel,
        out_shape=(
            jax.ShapeDtypeStruct((1, 2, ROWS, COLS, CH), BF16),
            jax.ShapeDtypeStruct((3, CH, CH), F32),
        ),
        in_specs=[hbm] * 6,
        out_specs=(vm, vm),
        scratch_shapes=scratch,
        compiler_params=pltpu.CompilerParams(
            collective_id=0, has_side_effects=True, vmem_limit_bytes=48 * 2**20
        ),
        name="block",
    )(
        *(
            pltpu.with_memory_space_constraint(v, pltpu.HBM)
            for v in (
                activations, norm_gain, norm_bias, spatial_weight, temporal_weight, cotangent,
            )
        )
    )


def solution(mesh):
    in_specs = (
        P("dp", "tm", None, None, "mp"),
        P("mp"),
        P("mp"),
        P(None, "mp", "tm"),
        P(None, "tm", "mp"),
        P("dp", "tm", None, None, "mp"),
    )
    out_specs = (P("dp", "tm", None, None, "mp"), P(None, "tm", "mp"))
    return jax.shard_map(body, mesh=mesh, in_specs=in_specs, out_specs=out_specs, check_vma=False)
```
